32 devices in a mesh: group: 4 (over y, x), member: 8 (over z, core).
Axes of the slice: x: 2, y: 2, z: 4, core: 2. Of those that a mesh axis runs over, the one named last changes fastest.
Arguments:
- factor: float32 [4, 16, 768, 768], P('group', 'member'), as said below
- load: float32 [4, 16, 768], P('group', 'member'), may hold values from -6 to 6
- dof_map: int32 [4, 16, 768], P('group', 'member'), may hold values from 0 to 767, as said below
- dof_sign: int32 [4, 16, 768], P('group', 'member'), may hold values from -1 to 1, as said below
- live_count: int32 [4, 16], P('group', 'member'), may hold values from 384 to 768, as said below
- face_slot: int32 [4, 16, 4, 64], P('group', 'member'), may hold values from 0 to 767, as said below
- face_count: int32 [4, 16, 4], P('group', 'member'), may hold values from 0 to 64, as said below
- node_coord: int32 [4, 16, 3, 256], P('group', 'member'), may hold values from 0 to 15
- coarse_inverse: float32 [384, 384], P(('group', 'member')), as said below
Outputs:
- multipliers: float32 [4, 16, 768], P('group', 'member')
- projected: float32 [4, 16, 768], P('group', 'member')
The draws below stay inside these ranges and needn't reach their ends.
Inputs may be any that keep to these rules, and one draw needn't show every extreme that they name: `dof_map`: each subdomain's row is a permutation of the unknowns. `dof_sign`: every entry is -1 or 1. `live_count`: in each cluster, both subdomains of one device have 768 live multipliers and both subdomains of the device whose member index differs by a quarter of 16 have 384. `face_slot`: the slots of one subdomain are distinct and below its live_count; slot k of a face pairs with slot k of the partner's face. `face_count`: A face and its partner's face have the same count; faces at the ends of a cluster's chain and at the first and last cluster have 0, all others 1 or more. `factor`: lower triangular with a positive diagonal. `coarse_inverse`: symmetric positive definite.
All inputs are finite; a program needn't handle non-finite values.
Results may differ from the reference program's by a relative error of at most 0.0003.
Values sent between devices are 32-bit elements; how exact they have to be, the bound alone decides.
A program may use at most 128 MiB of HBM per device.

```python
import jax
import jax.numpy as jnp
from jax import lax

NDOF = 768
NODES = 256
MODES = 6
CAP = 64
LIVE_MIN = 384
ITERS = 3
CLUSTERS = 4
SUBS = 16
COARSE = 384


def geometry(key):
    key_list = jax.random.split(jax.random.fold_in(key, 4242), 12)
    count_subs = CLUSTERS * SUBS
    dof_maps = jax.vmap(lambda sub_key: jax.random.permutation(sub_key, NDOF))(jax.random.split(key_list[0], count_subs))
    dof_maps = dof_maps.astype(jnp.int32).reshape(CLUSTERS, SUBS, NDOF)
    dof_signs = (2 * jax.random.randint(key_list[1], (CLUSTERS, SUBS, NDOF), 0, 2) - 1).astype(jnp.int32)
    trials = jax.random.randint(key_list[2], (3, CLUSTERS, SUBS), 0, NDOF - LIVE_MIN + 1)
    live_counts = LIVE_MIN + jnp.min(trials, axis=0)
    members = SUBS // 2
    heavy_member = jax.random.randint(key_list[3], (CLUSTERS, 1), 0, members)
    light_member = (heavy_member + members // 2) % members
    member_index = (jnp.arange(SUBS, dtype=jnp.int32) // 2)[None, :]
    live_counts = jnp.where(member_index == heavy_member, NDOF, live_counts)
    live_counts = jnp.where(member_index == light_member, LIVE_MIN, live_counts).astype(jnp.int32)
    along_counts = jnp.minimum(jax.random.randint(key_list[4], (CLUSTERS, SUBS - 1), 1, CAP + 1), jax.random.randint(key_list[5], (CLUSTERS, SUBS - 1), 1, CAP + 1))
    forced_along = jax.random.randint(key_list[6], (), 0, CLUSTERS * (SUBS - 1))
    along_index = jnp.arange(CLUSTERS * (SUBS - 1), dtype=jnp.int32).reshape(CLUSTERS, SUBS - 1)
    along_counts = jnp.where(along_index == forced_along, CAP, along_counts)
    across_counts = jnp.minimum(jax.random.randint(key_list[7], (CLUSTERS - 1, SUBS), 1, CAP + 1), jax.random.randint(key_list[8], (CLUSTERS - 1, SUBS), 1, CAP + 1))
    forced_across = jax.random.randint(key_list[9], (), 0, (CLUSTERS - 1) * SUBS)
    across_index = jnp.arange((CLUSTERS - 1) * SUBS, dtype=jnp.int32).reshape(CLUSTERS - 1, SUBS)
    across_counts = jnp.where(across_index == forced_across, CAP, across_counts)
    zero_col = jnp.zeros((CLUSTERS, 1), jnp.int32)
    zero_row = jnp.zeros((1, SUBS), jnp.int32)
    face_counts = jnp.stack([jnp.concatenate([zero_col, along_counts], axis=1), jnp.concatenate([along_counts, zero_col], axis=1), jnp.concatenate([zero_row, across_counts], axis=0), jnp.concatenate([across_counts, zero_row], axis=0)], axis=2).astype(jnp.int32)
    positions = jnp.arange(NDOF, dtype=jnp.int32)
    raw_rank = jax.random.randint(key_list[10], (CLUSTERS, SUBS, NDOF), 0, 2 ** 20)
    sub_grid = jnp.arange(SUBS, dtype=jnp.int32)[None, :, None]
    clu_grid = jnp.arange(CLUSTERS, dtype=jnp.int32)[:, None, None]
    chosen_sub = 2 * heavy_member[0, 0]
    force_last = (clu_grid == 0) & (sub_grid == chosen_sub) & (positions[None, None, :] == NDOF - 1)
    raw_rank = jnp.where(force_last, 0, raw_rank)
    scores = raw_rank * NDOF + positions
    scores = jnp.where(positions[None, None, :] < live_counts[:, :, None], scores, 2000000000 + positions)
    ordering = jnp.argsort(scores, axis=2, stable=True).astype(jnp.int32)
    slot_list = ordering[:, :, :4 * CAP].reshape(CLUSTERS, SUBS, 4, CAP)
    coordinates = jax.random.randint(key_list[11], (CLUSTERS, SUBS, 3, NODES), 0, 16).astype(jnp.int32)
    return (dof_maps, dof_signs, live_counts, face_counts, slot_list, coordinates)


def draw_dof_map(key, part):
    return geometry(key)[0]


def draw_dof_sign(key, part):
    return geometry(key)[1]


def draw_live_count(key, part):
    return geometry(key)[2]


def draw_face_count(key, part):
    return geometry(key)[3]


def draw_face_slot(key, part):
    return geometry(key)[4]


def draw_node_coord(key, part):
    return geometry(key)[5]


def draw_factor(key, part):
    key_diag, key_lower, key_band, key_sign = jax.random.split(jax.random.fold_in(key, 9100), 4)
    diag_log = jax.random.uniform(key_diag, (CLUSTERS, SUBS, NDOF), jnp.float32, jnp.log(2.5), jnp.log(7.5))
    rough = jax.random.normal(key_lower, (CLUSTERS, SUBS, NDOF, NDOF), jnp.float32)
    band_size = jax.random.uniform(key_band, (CLUSTERS, SUBS, NDOF), jnp.float32, 0.9, 0.97)
    band_sign = (2 * jax.random.randint(key_sign, (CLUSTERS, SUBS, NDOF), 0, 2) - 1).astype(jnp.float32)
    below = jnp.eye(NDOF, k=-1, dtype=jnp.float32)
    band_part = (band_sign * band_size)[..., :, None] * below
    lower_part = jnp.tril(rough, -1) * (0.35 / jnp.sqrt(float(NDOF)))
    unit_lower = lower_part + band_part + jnp.eye(NDOF, dtype=jnp.float32)
    return jnp.exp(diag_log)[..., :, None] * unit_lower


def draw_coarse_inverse(key, part):
    key_rate, key_gain = jax.random.split(jax.random.fold_in(key, 7300))
    subs_total = CLUSTERS * SUBS
    rates = jnp.exp(jax.random.uniform(key_rate, (MODES,), jnp.float32, jnp.log(0.5), jnp.log(3.0)))
    gains = jnp.exp(jax.random.uniform(key_gain, (COARSE,), jnp.float32, jnp.log(0.6), jnp.log(1.6)))
    index = jnp.arange(COARSE, dtype=jnp.int32)
    sub_index = (index // MODES).astype(jnp.float32)
    mode_index = index % MODES
    same_mode = (mode_index[:, None] == mode_index[None, :]).astype(jnp.float32)
    distance = jnp.abs(sub_index[:, None] - sub_index[None, :]) / float(subs_total)
    rate_row = rates[mode_index][:, None]
    kernel = jnp.exp(-rate_row * distance) * same_mode
    scale = 4.0 / (float(NDOF) * jnp.sqrt(float(subs_total)))
    return scale * gains[:, None] * gains[None, :] * kernel


def shard_levels(key, dims, cuts, low, high):
    loudness, own = 1.0, jax.random.fold_in(key, 6)
    for axis_at, parts in cuts:
        draws = jnp.exp(jax.random.uniform(jax.random.fold_in(own, axis_at), (parts,), jnp.float32, low / len(cuts), high / len(cuts)))
        loudness = loudness * jnp.repeat(draws, dims[axis_at] // parts).reshape([-1 if axis == axis_at else 1 for axis in range(len(dims))])
    return loudness


def normal_values(own_key, shape, scale, most, cuts=(), held_as=jnp.bfloat16):
    loudness = shard_levels(own_key, shape, cuts, -0.22, 0.18) if cuts else 1.0
    values = jax.random.normal(own_key, shape, jnp.float32) * scale * loudness
    return jnp.minimum(jnp.maximum(values, -most), most).astype(held_as)


def setup_inputs(seed: int = 0) -> dict:
    arg_keys = jax.random.split(jax.random.key(seed), 10)
    return {
        "factor": draw_factor(jax.random.fold_in(arg_keys[9], 71), 0),
        "load": normal_values(arg_keys[1], (CLUSTERS, SUBS, NDOF), 1.0, 6.0, ((0, 4), (1, 8)), jnp.float32),
        "dof_map": draw_dof_map(jax.random.fold_in(arg_keys[9], 71), 0),
        "dof_sign": draw_dof_sign(jax.random.fold_in(arg_keys[9], 71), 0),
        "live_count": draw_live_count(jax.random.fold_in(arg_keys[9], 71), 0),
        "face_slot": draw_face_slot(jax.random.fold_in(arg_keys[9], 71), 0),
        "face_count": draw_face_count(jax.random.fold_in(arg_keys[9], 71), 0),
        "node_coord": draw_node_coord(jax.random.fold_in(arg_keys[9], 71), 0),
        "coarse_inverse": draw_coarse_inverse(jax.random.fold_in(arg_keys[9], 71), 0),
    }


highest = lax.Precision.HIGHEST
half_span = 8.0

def rigid_modes(node_coord):
    position = (node_coord.astype(jnp.float32) - half_span) / half_span
    spread = jnp.repeat(position, 3, axis=-1)
    component = jnp.arange(spread.shape[-1], dtype=jnp.int32) % 3
    first = (component == 0).astype(spread.dtype)
    second = (component == 1).astype(spread.dtype)
    third = (component == 2).astype(spread.dtype)
    coord_x = spread[..., 0, :]
    coord_y = spread[..., 1, :]
    coord_z = spread[..., 2, :]
    unit_row = jnp.ones_like(coord_x)
    return jnp.stack([first * unit_row, second * unit_row, third * unit_row, third * coord_y - second * coord_z, first * coord_z - third * coord_x, second * coord_x - first * coord_y], axis=-2)

def add_into(values, slot_list, amounts):
    flat_values = values.reshape(-1, values.shape[-1])
    rows = flat_values.shape[0]
    result = jax.vmap(lambda row_values, row_slots, row_amounts: row_values.at[row_slots].add(row_amounts))(flat_values, slot_list.reshape(rows, -1), amounts.reshape(rows, -1))
    return result.reshape(values.shape)

def reference(factor, load, dof_map, dof_sign, live_count, face_slot, face_count, node_coord, coarse_inverse):
    positions = jnp.arange(NDOF, dtype=jnp.int32)
    live_mask = positions[None, None, :] < live_count[:, :, None]
    signed = jnp.where(live_mask, dof_sign, 0).astype(jnp.float32)
    count_subs = CLUSTERS * SUBS
    panels = factor.reshape(count_subs, NDOF, NDOF)

    def one_dual(inputs):
        panel_matrix, mapping, sign_row = inputs
        inverse = lax.linalg.triangular_solve(panel_matrix, jnp.eye(NDOF, dtype=panel_matrix.dtype), left_side=True, lower=True)
        columns = jnp.take(inverse, mapping, axis=1) * sign_row[None, :]
        return jnp.dot(columns.T, columns, precision=highest)
    dual_all = lax.map(one_dual, (panels, dof_map.reshape(count_subs, NDOF), signed.reshape(count_subs, NDOF)))
    dual_all = dual_all.reshape(CLUSTERS, SUBS, NDOF, NDOF)

    def one_gap(inputs):
        panel_matrix, load_row = inputs
        forward = lax.linalg.triangular_solve(panel_matrix, load_row[:, None], left_side=True, lower=True)
        backward = lax.linalg.triangular_solve(panel_matrix, forward, left_side=True, lower=True, transpose_a=True)
        return backward[:, 0]
    displaced = lax.map(one_gap, (panels, load.reshape(count_subs, NDOF))).reshape(CLUSTERS, SUBS, NDOF)
    gap_local = jnp.take_along_axis(displaced, dof_map, axis=2) * signed
    mode_table = rigid_modes(node_coord)
    rigid_rows = jnp.take_along_axis(mode_table, jnp.broadcast_to(dof_map[:, :, None, :], mode_table.shape), axis=3)
    rigid_rows = rigid_rows * signed[:, :, None, :]
    coarse_rhs = jnp.einsum('gsai,gsi->gsa', mode_table, load, precision=highest)
    slot_used = (jnp.arange(CAP, dtype=jnp.int32)[None, None, None, :] < face_count[..., None]).astype(jnp.float32)
    flat_slots = face_slot.reshape(CLUSTERS, SUBS, 4 * CAP)
    shared = add_into(jnp.zeros_like(gap_local), flat_slots, slot_used.reshape(CLUSTERS, SUBS, 4 * CAP))
    weight = live_mask.astype(jnp.float32) * (1.0 - 0.5 * shared)

    def assemble(values):
        outgoing = jnp.take_along_axis(values, flat_slots, axis=2).reshape(CLUSTERS, SUBS, 4, CAP) * slot_used
        empty_row = jnp.zeros_like(outgoing[:, :1, 0])
        from_left = jnp.concatenate([empty_row, outgoing[:, :-1, 1]], axis=1)
        from_right = jnp.concatenate([outgoing[:, 1:, 0], empty_row], axis=1)
        empty_col = jnp.zeros_like(outgoing[:1, :, 0])
        from_below = jnp.concatenate([empty_col, outgoing[:-1, :, 3]], axis=0)
        from_above = jnp.concatenate([outgoing[1:, :, 2], empty_col], axis=0)
        incoming = jnp.stack([from_left, from_right, from_below, from_above], axis=2) * slot_used
        return add_into(values, flat_slots, incoming.reshape(CLUSTERS, SUBS, 4 * CAP))

    def inner(left_field, right_field):
        return jnp.sum(weight * left_field * right_field)

    def apply_inverse(coarse):
        return jnp.dot(coarse_inverse, coarse.reshape(COARSE), precision=highest).reshape(CLUSTERS, SUBS, MODES)

    def spread_modes(alpha):
        return jnp.einsum('gsaj,gsa->gsj', rigid_rows, alpha, precision=highest)

    def project(values):
        coarse = jnp.einsum('gsaj,gsj->gsa', rigid_rows, values, precision=highest)
        return values - assemble(spread_modes(apply_inverse(coarse)))

    def apply_dual(values):
        return jnp.einsum('gsij,gsj->gsi', dual_all, values, precision=highest)
    multipliers = assemble(spread_modes(apply_inverse(coarse_rhs)))
    residual = assemble(gap_local - apply_dual(multipliers))
    projected = project(residual)
    direction = projected
    norm_now = inner(projected, projected)
    for iteration in range(ITERS):
        image_vec = assemble(apply_dual(direction))
        step_size = norm_now / inner(direction, image_vec)
        multipliers = multipliers + step_size * direction
        residual = residual - step_size * image_vec
        projected = project(residual)
        norm_next = inner(projected, projected)
        direction = projected + norm_next / norm_now * direction
        norm_now = norm_next
    return (multipliers, projected)
```

```python
import functools

import jax
import jax.numpy as jnp
from jax import lax
from jax.experimental import pallas as pl
from jax.experimental.pallas import tpu as pltpu
from jax.sharding import PartitionSpec as P

ITERS = 3
BASE = 16
TILE = 128
HALF_SPAN = 8.0
LEFT, RIGHT, DOWN, UP = range(4)
F32 = jnp.float32
BF16 = jnp.bfloat16
NT = (((1,), (1,)), ((), ()))
NN = (((1,), (0,)), ((), ()))


def iota(shape, dim):
    return lax.broadcasted_iota(jnp.int32, shape, dim)


def dot(left, right, dims=NN):
    return lax.dot_general(left, right, dims, preferred_element_type=F32)


def parts_of(values, count):
    parts = []
    for _ in range(count):
        part = values.astype(BF16)
        parts.append(part)
        values = values - part.astype(F32)
    return parts


def mm(left, right):
    left_hi, left_lo = parts_of(left, 2)
    right_hi, right_lo = parts_of(right, 2)
    return dot(left_hi, right_hi) + (dot(left_hi, right_lo) + dot(left_lo, right_hi))


def row_times(rows, table, dims=NN):
    stacked = []
    for row in rows:
        for part in parts_of(row, 3):
            stacked.append(part.astype(F32))
    pad = -len(stacked) % 8
    stacked.append(jnp.zeros((pad, rows[0].shape[1]), F32))
    product = dot(jnp.concatenate(stacked, axis=0).astype(BF16), table, dims)
    return [
        product[3 * at : 3 * at + 1] + product[3 * at + 1 : 3 * at + 2] + product[3 * at + 2 : 3 * at + 3]
        for at in range(len(rows))
    ]


def invert(factor, linv, subs):
    size = factor.shape[1]
    blocks = size // TILE
    row = iota((TILE, TILE), 0)
    lane = iota((TILE, TILE), 1)
    shift = BASE.bit_length() - 1
    same = (row >> shift) == (lane >> shift)
    where_at = [(s, b) for s in range(subs) for b in range(blocks)]

    def diagonal(s, b):
        return factor[s, b * TILE : (b + 1) * TILE, b * TILE : (b + 1) * TILE]

    packed = []
    for s, b in where_at:
        kept = jnp.where(same, diagonal(s, b), 0.0)
        packed.append(jnp.sum(kept.reshape(TILE // BASE, BASE, TILE), axis=0))
    count = len(packed)
    packed = jnp.concatenate(packed, axis=0)
    wide = (TILE, BASE * TILE)
    source, target = iota(wide, 0), iota(wide, 1)
    spread = (((source & (BASE - 1)) == (target >> 7)) & ((source >> shift) == ((target & 127) >> shift)))
    spread = jnp.where(spread, 1.0, 0.0).astype(BF16)
    columns = sum(dot(part, spread) for part in parts_of(packed, 3))
    within = iota((count, BASE, TILE), 1)
    solved = jnp.where(within == (iota((count, BASE, TILE), 2) & (BASE - 1)), 1.0, 0.0)
    for m in range(BASE):
        column = columns[:, m * TILE : (m + 1) * TILE].reshape(count, BASE, TILE)
        pivot = solved[:, m : m + 1, :] / column[:, m : m + 1, :]
        solved = jnp.where(within > m, solved - column * pivot, jnp.where(within == m, pivot, solved))
    inverses = [
        jnp.where(same, jnp.concatenate([solved[at]] * (TILE // BASE), axis=0), 0.0) for at in range(count)
    ]
    width = BASE
    while width < TILE:
        level = width.bit_length() - 1
        below = (
            ((row >> (level + 1)) == (lane >> (level + 1)))
            & (((row >> level) & 1) == 1)
            & (((lane >> level) & 1) == 0)
        )
        middle = [
            mm(jnp.where(below, diagonal(s, b), 0.0), inverses[at]) for at, (s, b) in enumerate(where_at)
        ]
        inverses = [inverses[at] - mm(inverses[at], middle[at]) for at in range(count)]
        width *= 2
    for at, (s, b) in enumerate(where_at):
        rows = slice(b * TILE, (b + 1) * TILE)
        linv[s, rows, rows] = inverses[at]
        if b + 1 < blocks:
            linv[s, rows, (b + 1) * TILE :] = jnp.zeros((TILE, size - (b + 1) * TILE), F32)
    width = TILE
    while width < size:
        for start in range(0, size - width, 2 * width):
            middle_at, end = start + width, min(start + 2 * width, size)
            for s in range(subs):
                upper = linv[s, start:middle_at, start:middle_at]
                lower = linv[s, middle_at:end, middle_at:end]
                linv[s, middle_at:end, start:middle_at] = -mm(lower, mm(factor[s, middle_at:end, start:middle_at], upper))
        width *= 2


def setup_kernel(
    live, face_count, factor, load, dof_map, dof_sign, face_slot, coord,
    linv, pack, unpack, slots, mask, weight, modes, face_modes, rhs,
):
    subs, size = load.shape
    cap = face_slot.shape[2]
    nodes = coord.shape[2]
    for s in range(subs):
        sign_row = jnp.where(iota((1, size), 1) < live[s], dof_sign[s : s + 1, :].astype(F32), 0.0)
        slot_rows = jnp.where(iota((size, size), 0) == dof_map[s : s + 1, :], sign_row, 0.0).astype(BF16)
        slots[s] = slot_rows

        def table_of(order):
            face_row = jnp.concatenate([face_slot[s, f : f + 1, :] for f in order], axis=1)
            lane = iota((1, 4 * cap), 1)
            limit = jnp.zeros((1, 4 * cap), jnp.int32)
            for at, f in enumerate(order):
                limit = jnp.where(lane // cap == at, at * cap + face_count[s, f], limit)
            face_row = jnp.where(lane < limit, face_row, -1)
            hit = jnp.where(iota((size, 4 * cap), 0) == face_row, 1.0, 0.0).astype(BF16)
            return dot(slot_rows, hit).astype(BF16)

        outgoing = table_of((0, 1, 2, 3))
        pack[s] = outgoing
        unpack[s] = table_of((1, 0, 3, 2))
        live_row = jnp.abs(dot(jnp.ones((8, size), BF16), slot_rows, NT))[0:1]
        shared = dot(jnp.ones((8, 4 * cap), BF16), jnp.abs(outgoing), NT)[0:1]
        mask[s : s + 1, :] = live_row
        weight[s : s + 1, :] = live_row * (1.0 - 0.5 * shared)
        position = (coord[s].astype(F32) - HALF_SPAN) / HALF_SPAN
        stacked = jnp.concatenate(
            [position, iota((1, nodes), 1).astype(F32), jnp.zeros((4, nodes), F32)], axis=0
        ).astype(BF16)
        first_of = 3 * iota((nodes, size), 0)
        unknown = iota((nodes, size), 1)
        of_node = jnp.where((unknown >= first_of) & (unknown < first_of + 3), 1.0, 0.0).astype(BF16)
        spread = dot(stacked, of_node)
        x, y, z = spread[0:1], spread[1:2], spread[2:3]
        component = iota((1, size), 1).astype(F32) - 3.0 * spread[3:4]
        first = jnp.where(component == 0.0, 1.0, 0.0)
        second = jnp.where(component == 1.0, 1.0, 0.0)
        third = jnp.where(component == 2.0, 1.0, 0.0)
        table = jnp.concatenate(
            [
                first,
                second,
                third,
                third * y - second * z,
                first * z - third * x,
                second * x - first * y,
                jnp.zeros((2, size), F32),
            ],
            axis=0,
        )
        modes[s] = table * live_row
        face_modes[s] = dot(table.astype(BF16), outgoing)
        rhs[s] = jnp.broadcast_to(jnp.sum(table * load[s : s + 1, :], axis=1, keepdims=True), (8, TILE))
    invert(factor, linv, subs)


def pcg_kernel(
    groups, members,
    linv, pack, unpack, slots, mask, weight, load, modes, face_modes, rhs, coarse,
    out_multipliers, out_projected,
    inverse_rows, face_in, shape_rows, gather_in, gather_out, halo_in, halo_out,
    send_gather, recv_gather, send_halo, recv_halo, send_setup, recv_setup,
):
    subs, size = load.shape
    faces = pack.shape[2]
    cap = faces // 4
    total = groups * members
    span = 16 * groups
    width = coarse.shape[-1]
    message = gather_out.shape[-1]
    c, m = lax.axis_index("group"), lax.axis_index("member")
    me = c * members + m
    neighbours = (
        (m > 0, (c, lax.rem(m + members - 1, members))),
        (m < members - 1, (c, lax.rem(m + 1, members))),
        (c > 0, (lax.rem(c + groups - 1, groups), m)),
        (c < groups - 1, (lax.rem(c + 1, groups), m)),
    )
    opposite = (RIGHT, LEFT, UP, DOWN)

    def peer(step):
        other = lax.rem(me + step, total)
        return (other // members, lax.rem(other, members))

    inverse_rows[...] = jnp.zeros(inverse_rows.shape, F32)
    face_in[...] = jnp.zeros(face_in.shape, F32)
    halo_in[...] = jnp.zeros(halo_in.shape, F32)

    barrier = pltpu.get_barrier_semaphore()

    @pl.loop(1, total)
    def _(step):
        pl.semaphore_signal(barrier, inc=1, device_id=peer(step), device_id_type=pl.DeviceIdType.MESH)

    pl.semaphore_wait(barrier, total - 1)

    def remote(src, dst, send, recv, where):
        return pltpu.make_async_remote_copy(
            src_ref=src, dst_ref=dst, send_sem=send, recv_sem=recv,
            device_id=where, device_id_type=pl.DeviceIdType.MESH,
        )

    def sided(ref, way):
        if way == LEFT:
            return ref.at[0]
        return ref.at[1] if way == RIGHT else ref

    def halo_copy(turn, way):
        to = opposite[way]
        return remote(
            sided(halo_out.at[turn], way), sided(halo_in.at[turn, to], way),
            send_halo.at[turn, way], recv_halo.at[turn, to], neighbours[way][1],
        )

    def face_copy(way):
        to = opposite[way]
        return remote(
            sided(face_modes, way), sided(face_in.at[to], way),
            send_setup.at[0, way], recv_setup.at[0, to], neighbours[way][1],
        )

    def coarse_copy(way):
        to = opposite[way]
        return remote(
            sided(coarse, way),
            (inverse_rows.at[2, 1], inverse_rows.at[1, 0], inverse_rows.at[4], inverse_rows.at[3])[way],
            send_setup.at[1, way], recv_setup.at[1, to], neighbours[way][1],
        )

    def each_way(action):
        for way in range(4):
            @pl.when(neighbours[way][0])
            def _():
                action(way)

    def gather_start(turn, row):
        gather_out[turn] = row
        gather_in[turn, me] = row

        @pl.loop(1, total)
        def _(step):
            remote(
                gather_out.at[turn], gather_in.at[turn, me],
                send_gather.at[turn], recv_gather.at[turn], peer(step),
            ).start()

    def gather_view(turn):
        return gather_in.at[turn, pl.ds(0, total - 1)]

    def gather_wait(turn):
        view = gather_view(turn)
        pltpu.make_async_copy(view, view, recv_gather.at[turn]).wait()

    lane_row = iota((1, message), 1)

    def placing(s):
        at = iota((40, message), 0)
        lane = iota((40, message), 1)
        kind, a = at >> 3, at & 7
        own = 16 * c + 8 * s
        to_left = own - 8 if s == 1 else span + 16 * c + 8
        to_right = own + 8 if s == 0 else span + 16 * c
        base = jnp.where(kind == 0, own, jnp.where(kind == 1, to_left, jnp.where(
            kind == 2, to_right, jnp.where(kind == 3, own - 16, own + 16))))
        return jnp.where((lane == base + a) & (a < 6), 1.0, 0.0)

    places = [placing(s) for s in range(subs)]

    def coarse_sum(turn):
        summed = jnp.sum(gather_in[turn].reshape(groups, members, 1, message), axis=0).reshape(members, message)
        if span >= TILE:
            low, high = summed[:, :span], summed[:, span : 2 * span]
        else:
            lane = iota((members, message), 1)
            low = jnp.where(lane < span, summed, 0.0)
            high = jnp.where(lane < span, pltpu.roll(summed, message - span, 1), 0.0)
        second = ((iota((members, width), 1) >> 3) & 1) == 1
        none = jnp.zeros((1, width), F32)
        from_right = jnp.concatenate([high[1:], none], axis=0)
        from_left = jnp.concatenate([none, high[:-1]], axis=0)
        return low + jnp.where(second, from_right, from_left)

    def correction(coarse_values):
        fields = []
        for s in range(subs):
            spread = jnp.zeros((8, size), F32)
            for kind in range(5):
                product = jnp.zeros((8, width), F32)
                for at in range(members):
                    product = product + inverse_rows[kind, s, at] * coarse_values[at : at + 1, :]
                alpha = jnp.sum(product, axis=1, keepdims=True)
                spread = spread + shape_rows[s, 8 * kind : 8 * kind + 8, :] * alpha
            fields.append(jnp.sum(spread, axis=0, keepdims=True))
        return fields

    def apply_dual(fields):
        images = []
        for s in range(subs):
            sums = [jnp.zeros((8, TILE), F32) for _ in range(size // TILE)]
            for b in range(size // TILE):
                reach = (b + 1) * TILE
                panel = linv[s, b * TILE : reach, :reach]
                column = jnp.sum(panel * fields[s][:, :reach], axis=1, keepdims=True)
                for at in range(b + 1):
                    piece = panel[:, at * TILE : (at + 1) * TILE] * column
                    sums[at] = sums[at] + jnp.sum(piece.reshape(TILE // 8, 8, TILE), axis=0)
            image = jnp.concatenate([jnp.sum(part, axis=0, keepdims=True) for part in sums], axis=1)
            images.append(image * mask[s : s + 1, :])
        return images

    face_lane = iota((1, faces), 1)

    def from_faces(right, left, up, down):
        return jnp.where(
            face_lane < cap, right,
            jnp.where(face_lane < 2 * cap, left, jnp.where(face_lane < 3 * cap, up, down)),
        )

    def project(turn, fields, scalars):
        outgoing = [row_times([fields[s]], pack[s])[0] for s in range(subs)]
        for s in range(subs):
            halo_out[turn - 1, s] = outgoing[s]
        each_way(lambda way: halo_copy(turn - 1, way).start())
        row = jnp.zeros((1, message), F32)
        for s in range(subs):
            column = jnp.sum(shape_rows[s] * fields[s], axis=1, keepdims=True)
            row = row + jnp.sum(places[s] * column, axis=0, keepdims=True)
        spare = (6, 7, 14)
        for at, value in enumerate(scalars):
            row = row + jnp.where(lane_row == 16 * c + spare[at], value, 0.0)
        gather_start(turn, row)
        each_way(lambda way: halo_copy(turn - 1, opposite[way]).wait_recv())
        arrived = halo_in.at[turn - 1]
        rights = (outgoing[1], arrived[RIGHT, 0])
        lefts = (arrived[LEFT, 1], outgoing[0])
        assembled = []
        for s in range(subs):
            incoming = from_faces(rights[s], lefts[s], arrived[UP, s], arrived[DOWN, s])
            assembled.append(fields[s] + row_times([incoming], unpack[s], NT)[0])
        gather_wait(turn)
        values = coarse_sum(turn)
        fixes = correction(values)
        spare_lane = iota(values.shape, 1) & 15
        sums = []
        for at in range(len(scalars)):
            kept = jnp.where(spare_lane == spare[at], values, 0.0)
            sums.append(jnp.sum(jnp.sum(kept, axis=1, keepdims=True), axis=0, keepdims=True))
        return [assembled[s] - fixes[s] for s in range(subs)], sums

    each_way(lambda way: face_copy(way).start())
    each_way(lambda way: coarse_copy(way).start())
    row = jnp.zeros((1, message), F32)
    for s in range(subs):
        column = jnp.concatenate([rhs[s][:, 0:1], jnp.zeros((32, 1), F32)], axis=0)
        row = row + jnp.sum(places[s] * column, axis=0, keepdims=True)
    gather_start(0, row)
    for s in range(subs):
        inverse_rows[0, s] = coarse[s]
    inverse_rows[2, 0] = coarse[1]
    inverse_rows[1, 1] = coarse[0]
    each_way(lambda way: face_copy(opposite[way]).wait_recv())
    each_way(lambda way: coarse_copy(opposite[way]).wait_recv())
    rights = (face_modes[1], face_in[RIGHT, 0])
    lefts = (face_in[LEFT, 1], face_modes[0])
    block = iota((8, faces), 1) // cap
    for s in range(subs):
        sources = (lefts[s], rights[s], face_in[DOWN, s], face_in[UP, s])
        spread = jnp.concatenate(
            [jnp.where(block == (1, 0, 3, 2)[f], sources[f], 0.0) for f in range(4)], axis=0
        ).astype(BF16)
        shape_rows[s, 0:8, :] = modes[s]
        shape_rows[s, 8:40, :] = dot(spread, unpack[s], NT)
    gather_wait(0)
    multipliers = correction(coarse_sum(0))
    start = apply_dual([load[s : s + 1, :] - multipliers[s] for s in range(subs)])
    projected, _ = project(1, start, [])
    for turn in range(ITERS):
        image = apply_dual(projected)
        norm = sum(
            jnp.sum(weight[s : s + 1, :] * projected[s] * projected[s], axis=1, keepdims=True) for s in range(subs)
        )
        energy = sum(jnp.sum(projected[s] * image[s], axis=1, keepdims=True) for s in range(subs))
        partials = [norm, energy]
        if turn:
            partials.append(
                sum(jnp.sum(projected[s] * direction_image[s], axis=1, keepdims=True) for s in range(subs))
            )
        change, sums = project(2 + turn, image, partials)
        if turn:
            ratio = sums[0] / norm_now
            curvature = sums[1] + 2.0 * ratio * sums[2] + ratio * ratio * curvature
            direction = [projected[s] + ratio * direction[s] for s in range(subs)]
            direction_image = [image[s] + ratio * direction_image[s] for s in range(subs)]
            direction_change = [change[s] + ratio * direction_change[s] for s in range(subs)]
        else:
            curvature = sums[1]
            direction, direction_image, direction_change = projected, image, change
        norm_now = sums[0]
        step = norm_now / curvature
        multipliers = [multipliers[s] + step * direction[s] for s in range(subs)]
        projected = [projected[s] - step * direction_change[s] for s in range(subs)]
    for s in range(subs):
        ordered = row_times([multipliers[s], projected[s]], slots[s])
        out_multipliers[s : s + 1, :] = ordered[0]
        out_projected[s : s + 1, :] = ordered[1]

    each_way(lambda way: face_copy(way).wait_send())
    each_way(lambda way: coarse_copy(way).wait_send())
    for turn in range(ITERS + 1):
        each_way(lambda way: halo_copy(turn, way).wait_send())
    for turn in range(ITERS + 2):
        view = gather_view(turn)
        pltpu.make_async_copy(view, view, send_gather.at[turn]).wait()


def shards(
    groups, members,
    factor, load, dof_map, dof_sign, live_count, face_slot, face_count, node_coord, coarse_inverse,
):
    subs, size = load.shape[1:]
    faces = 4 * face_slot.shape[3]
    span = 16 * groups
    width = -(-span // TILE) * TILE
    message = -(-2 * span // TILE) * TILE
    vmem = pl.BlockSpec(memory_space=pltpu.VMEM)
    smem = pl.BlockSpec(memory_space=pltpu.SMEM)
    shape = jax.ShapeDtypeStruct
    prepared = pl.pallas_call(
        setup_kernel,
        name="setup",
        out_shape=(
            shape((subs, size, size), F32),
            shape((subs, size, faces), BF16),
            shape((subs, size, faces), BF16),
            shape((subs, size, size), BF16),
            shape((subs, size), F32),
            shape((subs, size), F32),
            shape((subs, 8, size), F32),
            shape((subs, 8, faces), F32),
            shape((subs, 8, TILE), F32),
        ),
        in_specs=[smem, smem] + [vmem] * 6,
        out_specs=[vmem] * 9,
        compiler_params=pltpu.CompilerParams(vmem_limit_bytes=48 * 2**20),
    )(
        live_count[0], face_count[0], factor[0], load[0], dof_map[0], dof_sign[0], face_slot[0], node_coord[0]
    )
    rows = coarse_inverse.reshape(subs, 6, groups, members, subs, 6)
    rows = jnp.pad(rows, ((0, 0), (0, 2), (0, 0), (0, 0), (0, 0), (0, 2)))
    rows = rows.transpose(0, 3, 1, 2, 4, 5).reshape(subs, members, 8, span)
    rows = jnp.pad(rows, ((0, 0), (0, 0), (0, 0), (0, width - span)))
    linv, pack, unpack, slots, mask, weight, modes, face_modes, rhs = prepared
    turns = ITERS + 2
    multipliers, projected = pl.pallas_call(
        functools.partial(pcg_kernel, groups, members),
        name="pcg",
        out_shape=(shape((subs, size), F32), shape((subs, size), F32)),
        in_specs=[vmem] * 11,
        out_specs=[vmem] * 2,
        scratch_shapes=[
            pltpu.VMEM((5, subs, members, 8, width), F32),
            pltpu.VMEM((4, subs, 8, faces), F32),
            pltpu.VMEM((subs, 40, size), F32),
            pltpu.VMEM((turns, groups * members, 1, message), F32),
            pltpu.VMEM((turns, 1, message), F32),
            pltpu.VMEM((turns - 1, 4, subs, 1, faces), F32),
            pltpu.VMEM((turns - 1, subs, 1, faces), F32),
            pltpu.SemaphoreType.DMA((turns,)),
            pltpu.SemaphoreType.DMA((turns,)),
            pltpu.SemaphoreType.DMA((turns - 1, 4)),
            pltpu.SemaphoreType.DMA((turns - 1, 4)),
            pltpu.SemaphoreType.DMA((2, 4)),
            pltpu.SemaphoreType.DMA((2, 4)),
        ],
        compiler_params=pltpu.CompilerParams(
            collective_id=0, has_side_effects=True, vmem_limit_bytes=48 * 2**20
        ),
    )(linv, pack, unpack, slots, mask, weight, load[0], modes, face_modes, rhs, rows)
    return multipliers[None], projected[None]


def solution(mesh):
    return jax.shard_map(
        functools.partial(shards, mesh.shape["group"], mesh.shape["member"]),
        mesh=mesh,
        in_specs=(
            P("group", "member", None, None),
            P("group", "member", None),
            P("group", "member", None),
            P("group", "member", None),
            P("group", "member"),
            P("group", "member", None, None),
            P("group", "member", None),
            P("group", "member", None, None),
            P(("group", "member"), None),
        ),
        out_specs=(P("group", "member", None), P("group", "member", None)),
        check_vma=False,
    )
```

```python
import functools

import jax
import jax.numpy as jnp
from jax import lax
from jax.experimental import pallas as pl
from jax.experimental.pallas import tpu as pltpu
from jax.sharding import PartitionSpec as P

ITERS = 3
BASE = 16
TILE = 128
HALF_SPAN = 8.0
VMEM_LIMIT = 62 * 2**20
LEFT, RIGHT, DOWN, UP = range(4)
F32 = jnp.float32
BF16 = jnp.bfloat16
NT = (((1,), (1,)), ((), ()))
NN = (((1,), (0,)), ((), ()))


def iota(shape, dim):
    return lax.broadcasted_iota(jnp.int32, shape, dim)


def dot(left, right, dims=NN):
    return lax.dot_general(left, right, dims, preferred_element_type=F32)


def parts_of(values, count):
    parts = []
    for _ in range(count):
        part = values.astype(BF16)
        parts.append(part)
        values = values - part.astype(F32)
    return parts


def mm(left, right):
    left_hi, left_lo = parts_of(left, 2)
    right_hi, right_lo = parts_of(right, 2)
    return dot(left_hi, right_hi) + (dot(left_hi, right_lo) + dot(left_lo, right_hi))


def row_times(rows, table, dims=NN):
    stacked = []
    for row in rows:
        for part in parts_of(row, 3):
            stacked.append(part.astype(F32))
    pad = -len(stacked) % 8
    stacked.append(jnp.zeros((pad, rows[0].shape[1]), F32))
    product = dot(jnp.concatenate(stacked, axis=0).astype(BF16), table, dims)
    return [
        product[3 * at : 3 * at + 1] + product[3 * at + 1 : 3 * at + 2] + product[3 * at + 2 : 3 * at + 3]
        for at in range(len(rows))
    ]


def invert(factor, linv, subs):
    size = factor.shape[1]
    blocks = size // TILE
    row = iota((TILE, TILE), 0)
    lane = iota((TILE, TILE), 1)
    shift = BASE.bit_length() - 1
    same = (row >> shift) == (lane >> shift)
    where_at = [(s, b) for s in range(subs) for b in range(blocks)]

    def diagonal(s, b):
        return factor[s, b * TILE : (b + 1) * TILE, b * TILE : (b + 1) * TILE]

    packed = []
    for s, b in where_at:
        kept = jnp.where(same, diagonal(s, b), 0.0)
        packed.append(jnp.sum(kept.reshape(TILE // BASE, BASE, TILE), axis=0))
    count = len(packed)
    packed = jnp.concatenate(packed, axis=0)
    wide = (TILE, BASE * TILE)
    source, target = iota(wide, 0), iota(wide, 1)
    spread = (((source & (BASE - 1)) == (target >> 7)) & ((source >> shift) == ((target & 127) >> shift)))
    spread = jnp.where(spread, 1.0, 0.0).astype(BF16)
    columns = sum(dot(part, spread) for part in parts_of(packed, 3))
    within = iota((count, BASE, TILE), 1)
    solved = jnp.where(within == (iota((count, BASE, TILE), 2) & (BASE - 1)), 1.0, 0.0)
    for m in range(BASE):
        column = columns[:, m * TILE : (m + 1) * TILE].reshape(count, BASE, TILE)
        pivot = solved[:, m : m + 1, :] / column[:, m : m + 1, :]
        solved = jnp.where(within > m, solved - column * pivot, jnp.where(within == m, pivot, solved))
    inverses = [
        jnp.where(same, jnp.concatenate([solved[at]] * (TILE // BASE), axis=0), 0.0) for at in range(count)
    ]
    width = BASE
    while width < TILE:
        level = width.bit_length() - 1
        below = (
            ((row >> (level + 1)) == (lane >> (level + 1)))
            & (((row >> level) & 1) == 1)
            & (((lane >> level) & 1) == 0)
        )
        middle = [
            mm(jnp.where(below, diagonal(s, b), 0.0), inverses[at]) for at, (s, b) in enumerate(where_at)
        ]
        inverses = [inverses[at] - mm(inverses[at], middle[at]) for at in range(count)]
        width *= 2
    for at, (s, b) in enumerate(where_at):
        rows = slice(b * TILE, (b + 1) * TILE)
        linv[s, rows, rows] = inverses[at]
        if b + 1 < blocks:
            linv[s, rows, (b + 1) * TILE :] = jnp.zeros((TILE, size - (b + 1) * TILE), F32)
    width = TILE
    while width < size:
        for start in range(0, size - width, 2 * width):
            middle_at, end = start + width, min(start + 2 * width, size)
            for s in range(subs):
                upper = linv[s, start:middle_at, start:middle_at]
                lower = linv[s, middle_at:end, middle_at:end]
                linv[s, middle_at:end, start:middle_at] = -mm(lower, mm(factor[s, middle_at:end, start:middle_at], upper))
        width *= 2


def tables(
    live, face_count, load, dof_map, dof_sign, face_slot, coord,
    pack, unpack, slots, mask, weight, modes, face_modes, rhs,
):
    subs, size = load.shape
    cap = face_slot.shape[2]
    nodes = coord.shape[2]
    for s in range(subs):
        sign_row = jnp.where(iota((1, size), 1) < live[0:1, s : s + 1], dof_sign[s : s + 1, :].astype(F32), 0.0)
        slot_rows = jnp.where(iota((size, size), 0) == dof_map[s : s + 1, :], sign_row, 0.0).astype(BF16)
        slots[s] = slot_rows

        def table_of(order):
            face_row = jnp.concatenate([face_slot[s, f : f + 1, :] for f in order], axis=1)
            lane = iota((1, 4 * cap), 1)
            limit = jnp.zeros((1, 4 * cap), jnp.int32)
            for at, f in enumerate(order):
                limit = jnp.where(lane // cap == at, at * cap + face_count[s : s + 1, f : f + 1], limit)
            face_row = jnp.where(lane < limit, face_row, -1)
            hit = jnp.where(iota((size, 4 * cap), 0) == face_row, 1.0, 0.0).astype(BF16)
            return dot(slot_rows, hit).astype(BF16)

        outgoing = table_of((0, 1, 2, 3))
        pack[s] = outgoing
        unpack[s] = table_of((1, 0, 3, 2))
        live_row = jnp.abs(dot(jnp.ones((8, size), BF16), slot_rows, NT))[0:1]
        shared = dot(jnp.ones((8, 4 * cap), BF16), jnp.abs(outgoing), NT)[0:1]
        mask[s : s + 1, :] = live_row
        weight[s : s + 1, :] = live_row * (1.0 - 0.5 * shared)
        position = jnp.concatenate([coord[axis, s : s + 1, :] for axis in range(3)], axis=0)
        position = (position.astype(F32) - HALF_SPAN) / HALF_SPAN
        stacked = jnp.concatenate(
            [position, iota((1, nodes), 1).astype(F32), jnp.zeros((4, nodes), F32)], axis=0
        ).astype(BF16)
        first_of = 3 * iota((nodes, size), 0)
        unknown = iota((nodes, size), 1)
        of_node = jnp.where((unknown >= first_of) & (unknown < first_of + 3), 1.0, 0.0).astype(BF16)
        spread = dot(stacked, of_node)
        x, y, z = spread[0:1], spread[1:2], spread[2:3]
        component = iota((1, size), 1).astype(F32) - 3.0 * spread[3:4]
        first = jnp.where(component == 0.0, 1.0, 0.0)
        second = jnp.where(component == 1.0, 1.0, 0.0)
        third = jnp.where(component == 2.0, 1.0, 0.0)
        table = jnp.concatenate(
            [
                first,
                second,
                third,
                third * y - second * z,
                first * z - third * x,
                second * x - first * y,
                jnp.zeros((2, size), F32),
            ],
            axis=0,
        )
        modes[s] = table * live_row
        face_modes[s] = dot(table.astype(BF16), outgoing)
        rhs[s] = jnp.broadcast_to(jnp.sum(table * load[s : s + 1, :], axis=1, keepdims=True), (8, TILE))


def coarse_layout(raw, coarse, groups, members):
    width = coarse.shape[-1]
    none = jnp.zeros((2, raw.shape[1]), F32)
    rows = jnp.concatenate([raw[0:6, :], none, raw[6:12, :], none], axis=0)
    stacked = jnp.concatenate([part.astype(F32) for part in parts_of(rows, 3)], axis=0).astype(BF16)

    def one(at, carry):
        lane = iota((1, width), 1)
        column = 12 * ((lane >> 4) * members + at) + 6 * ((lane >> 3) & 1) + (lane & 7)
        column = jnp.where(((lane & 7) < 6) & (lane < 16 * groups), column, -1)
        pick = jnp.where(iota((raw.shape[1], width), 0) == column, 1.0, 0.0).astype(BF16)
        picked = dot(stacked, pick)
        picked = picked[0:16] + picked[16:32] + picked[32:48]
        coarse[0, at] = picked[0:8]
        coarse[1, at] = picked[8:16]
        return carry

    lax.fori_loop(0, members, one, 0, unroll=members <= 8)


def pcg_kernel(
    groups, members,
    factor_hbm, load_hbm, dof_map_hbm, dof_sign_hbm, live_hbm, face_slot_hbm, face_count_hbm, coord_hbm, raw_hbm,
    out_multipliers, out_projected,
    factor_own, load_own, dof_map_own, dof_sign_own, live_own, face_slot_own, face_count_own, coord_own, raw_own,
    linv, pack, unpack, slots, mask, weight, modes, face_modes, rhs, coarse, load_sem,
    inverse_rows, face_in, shape_rows, gather_in, gather_out, halo_in, halo_out,
    send_gather, recv_gather, send_halo, recv_halo, send_setup, recv_setup,
):
    loads = [
        pltpu.make_async_copy(src, dst, load_sem.at[at])
        for at, (src, dst) in enumerate((
            (load_hbm, load_own), (dof_map_hbm, dof_map_own), (dof_sign_hbm, dof_sign_own),
            (live_hbm, live_own), (face_slot_hbm, face_slot_own), (face_count_hbm, face_count_own),
            (coord_hbm, coord_own), (raw_hbm, raw_own), (factor_hbm, factor_own),
        ))
    ]
    for copy in loads:
        copy.start()
    factor, load = factor_own.at[0], load_own.at[0]
    subs, size = load.shape
    faces = pack.shape[2]
    cap = faces // 4
    total = groups * members
    span = 16 * groups
    width = coarse.shape[-1]
    message = gather_out.shape[-1]
    c, m = lax.axis_index("group"), lax.axis_index("member")
    me = c * members + m
    neighbours = (
        (m > 0, (c, lax.rem(m + members - 1, members))),
        (m < members - 1, (c, lax.rem(m + 1, members))),
        (c > 0, (lax.rem(c + groups - 1, groups), m)),
        (c < groups - 1, (lax.rem(c + 1, groups), m)),
    )
    opposite = (RIGHT, LEFT, UP, DOWN)

    across = [lax.rem(c + step, groups) for step in range(groups)]
    along = [lax.rem(m + step, members) for step in range(members)]

    def each_peer(action):
        if total <= 32:
            for far in range(members - 1, -1, -1):
                for off in range(groups - 1, -1, -1):
                    if far or off:
                        action((across[off], along[far]))
        else:
            @pl.loop(1, total)
            def _(step):
                other = lax.rem(me + step, total)
                action((other // members, lax.rem(other, members)))

    inverse_rows[...] = jnp.zeros(inverse_rows.shape, F32)
    face_in[...] = jnp.zeros(face_in.shape, F32)
    halo_in[...] = jnp.zeros(halo_in.shape, F32)

    barrier = pltpu.get_barrier_semaphore()

    each_peer(
        lambda where: pl.semaphore_signal(barrier, inc=1, device_id=where, device_id_type=pl.DeviceIdType.MESH)
    )
    for copy in loads[:-1]:
        copy.wait()
    tables(
        live_own, face_count_own.at[0], load, dof_map_own.at[0], dof_sign_own.at[0], face_slot_own.at[0],
        coord_own.at[0], pack, unpack, slots, mask, weight, modes, face_modes, rhs,
    )
    coarse_layout(raw_own, coarse, groups, members)
    pl.semaphore_wait(barrier, total - 1)

    def remote(src, dst, send, recv, where):
        return pltpu.make_async_remote_copy(
            src_ref=src, dst_ref=dst, send_sem=send, recv_sem=recv,
            device_id=where, device_id_type=pl.DeviceIdType.MESH,
        )

    def sided(ref, way):
        if way == LEFT:
            return ref.at[0]
        return ref.at[1] if way == RIGHT else ref

    def halo_copy(turn, way):
        to = opposite[way]
        return remote(
            sided(halo_out.at[turn], way), sided(halo_in.at[turn, to], way),
            send_halo.at[turn, way], recv_halo.at[turn, to], neighbours[way][1],
        )

    def face_copy(way):
        to = opposite[way]
        return remote(
            sided(face_modes, way), sided(face_in.at[to], way),
            send_setup.at[0, way], recv_setup.at[0, to], neighbours[way][1],
        )

    def coarse_copy(way):
        to = opposite[way]
        return remote(
            sided(coarse, way),
            (inverse_rows.at[2, 1], inverse_rows.at[1, 0], inverse_rows.at[4], inverse_rows.at[3])[way],
            send_setup.at[1, way], recv_setup.at[1, to], neighbours[way][1],
        )

    def each_way(action):
        for way in range(4):
            @pl.when(neighbours[way][0])
            def _():
                action(way)

    def gather_start(turn, row):
        gather_out[turn] = row
        gather_in[turn, me] = row

        each_peer(
            lambda where: remote(
                gather_out.at[turn], gather_in.at[turn, me],
                send_gather.at[turn], recv_gather.at[turn], where,
            ).start()
        )

    def gather_view(turn):
        return gather_in.at[turn, pl.ds(0, total - 1)]

    def gather_wait(turn):
        view = gather_view(turn)
        pltpu.make_async_copy(view, view, recv_gather.at[turn]).wait()

    lane_row = iota((1, message), 1)

    def placing(s):
        at = iota((40, message), 0)
        lane = iota((40, message), 1)
        kind, a = at >> 3, at & 7
        own = 16 * c + 8 * s
        to_left = own - 8 if s == 1 else span + 16 * c + 8
        to_right = own + 8 if s == 0 else span + 16 * c
        base = jnp.where(kind == 0, own, jnp.where(kind == 1, to_left, jnp.where(
            kind == 2, to_right, jnp.where(kind == 3, own - 16, own + 16))))
        return jnp.where((lane == base + a) & (a < 6), 1.0, 0.0)

    places = [placing(s) for s in range(subs)]

    def coarse_sum(turn):
        summed = jnp.sum(gather_in[turn].reshape(groups, members, 1, message), axis=0).reshape(members, message)
        if span >= TILE:
            low, high = summed[:, :span], summed[:, span : 2 * span]
        else:
            lane = iota((members, message), 1)
            low = jnp.where(lane < span, summed, 0.0)
            high = jnp.where(lane < span, pltpu.roll(summed, message - span, 1), 0.0)
        second = ((iota((members, width), 1) >> 3) & 1) == 1
        none = jnp.zeros((1, width), F32)
        from_right = jnp.concatenate([high[1:], none], axis=0)
        from_left = jnp.concatenate([none, high[:-1]], axis=0)
        return low + jnp.where(second, from_right, from_left)

    def correction(coarse_values):
        fields = []
        for s in range(subs):
            spread = jnp.zeros((8, size), F32)
            for kind in range(5):
                product = jnp.zeros((8, width), F32)
                for at in range(members):
                    product = product + inverse_rows[kind, s, at] * coarse_values[at : at + 1, :]
                alpha = jnp.sum(product, axis=1, keepdims=True)
                spread = spread + shape_rows[s, 8 * kind : 8 * kind + 8, :] * alpha
            fields.append(jnp.sum(spread, axis=0, keepdims=True))
        return fields

    def apply_dual(fields):
        images = []
        for s in range(subs):
            sums = [jnp.zeros((8, TILE), F32) for _ in range(size // TILE)]
            for b in range(size // TILE):
                reach = (b + 1) * TILE
                panel = linv[s, b * TILE : reach, :reach]
                column = jnp.sum(panel * fields[s][:, :reach], axis=1, keepdims=True)
                for at in range(b + 1):
                    piece = panel[:, at * TILE : (at + 1) * TILE] * column
                    sums[at] = sums[at] + jnp.sum(piece.reshape(TILE // 8, 8, TILE), axis=0)
            image = jnp.concatenate([jnp.sum(part, axis=0, keepdims=True) for part in sums], axis=1)
            images.append(image * mask[s : s + 1, :])
        return images

    face_lane = iota((1, faces), 1)

    def from_faces(right, left, up, down):
        return jnp.where(
            face_lane < cap, right,
            jnp.where(face_lane < 2 * cap, left, jnp.where(face_lane < 3 * cap, up, down)),
        )

    def project(turn, fields, scalars):
        outgoing = [row_times([fields[s]], pack[s])[0] for s in range(subs)]
        for s in range(subs):
            halo_out[turn - 1, s] = outgoing[s]
        each_way(lambda way: halo_copy(turn - 1, way).start())
        row = jnp.zeros((1, message), F32)
        for s in range(subs):
            column = jnp.sum(shape_rows[s] * fields[s], axis=1, keepdims=True)
            row = row + jnp.sum(places[s] * column, axis=0, keepdims=True)
        spare = (6, 7, 14)
        for at, value in enumerate(scalars):
            row = row + jnp.where(lane_row == 16 * c + spare[at], value, 0.0)
        gather_start(turn, row)
        each_way(lambda way: halo_copy(turn - 1, opposite[way]).wait_recv())
        arrived = halo_in.at[turn - 1]
        rights = (outgoing[1], arrived[RIGHT, 0])
        lefts = (arrived[LEFT, 1], outgoing[0])
        assembled = []
        for s in range(subs):
            incoming = from_faces(rights[s], lefts[s], arrived[UP, s], arrived[DOWN, s])
            assembled.append(fields[s] + row_times([incoming], unpack[s], NT)[0])
        gather_wait(turn)
        values = coarse_sum(turn)
        fixes = correction(values)
        spare_lane = iota(values.shape, 1) & 15
        sums = []
        for at in range(len(scalars)):
            kept = jnp.where(spare_lane == spare[at], values, 0.0)
            sums.append(jnp.sum(jnp.sum(kept, axis=1, keepdims=True), axis=0, keepdims=True))
        return [assembled[s] - fixes[s] for s in range(subs)], sums

    each_way(lambda way: face_copy(way).start())
    each_way(lambda way: coarse_copy(way).start())
    row = jnp.zeros((1, message), F32)
    for s in range(subs):
        column = jnp.concatenate([rhs[s][:, 0:1], jnp.zeros((32, 1), F32)], axis=0)
        row = row + jnp.sum(places[s] * column, axis=0, keepdims=True)
    gather_start(0, row)
    for s in range(subs):
        inverse_rows[0, s] = coarse[s]
    inverse_rows[2, 0] = coarse[1]
    inverse_rows[1, 1] = coarse[0]
    loads[-1].wait()
    invert(factor, linv, subs)
    each_way(lambda way: face_copy(opposite[way]).wait_recv())
    each_way(lambda way: coarse_copy(opposite[way]).wait_recv())
    rights = (face_modes[1], face_in[RIGHT, 0])
    lefts = (face_in[LEFT, 1], face_modes[0])
    block = iota((8, faces), 1) // cap
    for s in range(subs):
        sources = (lefts[s], rights[s], face_in[DOWN, s], face_in[UP, s])
        spread = jnp.concatenate(
            [jnp.where(block == (1, 0, 3, 2)[f], sources[f], 0.0) for f in range(4)], axis=0
        ).astype(BF16)
        shape_rows[s, 0:8, :] = modes[s]
        shape_rows[s, 8:40, :] = dot(spread, unpack[s], NT)
    gather_wait(0)
    multipliers = correction(coarse_sum(0))
    start = apply_dual([load[s : s + 1, :] - multipliers[s] for s in range(subs)])
    projected, _ = project(1, start, [])
    for turn in range(ITERS):
        image = apply_dual(projected)
        norm = sum(
            jnp.sum(weight[s : s + 1, :] * projected[s] * projected[s], axis=1, keepdims=True) for s in range(subs)
        )
        energy = sum(jnp.sum(projected[s] * image[s], axis=1, keepdims=True) for s in range(subs))
        partials = [norm, energy]
        if turn:
            partials.append(
                sum(jnp.sum(projected[s] * direction_image[s], axis=1, keepdims=True) for s in range(subs))
            )
        change, sums = project(2 + turn, image, partials)
        if turn:
            ratio = sums[0] / norm_now
            curvature = sums[1] + 2.0 * ratio * sums[2] + ratio * ratio * curvature
            direction = [projected[s] + ratio * direction[s] for s in range(subs)]
            direction_image = [image[s] + ratio * direction_image[s] for s in range(subs)]
            direction_change = [change[s] + ratio * direction_change[s] for s in range(subs)]
        else:
            curvature = sums[1]
            direction, direction_image, direction_change = projected, image, change
        norm_now = sums[0]
        step = norm_now / curvature
        multipliers = [multipliers[s] + step * direction[s] for s in range(subs)]
        projected = [projected[s] - step * direction_change[s] for s in range(subs)]
    for s in range(subs):
        ordered = row_times([multipliers[s], projected[s]], slots[s])
        out_multipliers[s : s + 1, :] = ordered[0]
        out_projected[s : s + 1, :] = ordered[1]

    each_way(lambda way: face_copy(way).wait_send())
    each_way(lambda way: coarse_copy(way).wait_send())
    for turn in range(ITERS + 1):
        each_way(lambda way: halo_copy(turn, way).wait_send())
    for turn in range(ITERS + 2):
        view = gather_view(turn)
        pltpu.make_async_copy(view, view, send_gather.at[turn]).wait()


def shards(
    groups, members,
    factor, load, dof_map, dof_sign, live_count, face_slot, face_count, node_coord, coarse_inverse,
):
    subs, size = load.shape[1:]
    faces = 4 * face_slot.shape[3]
    span = 16 * groups
    width = -(-span // TILE) * TILE
    message = -(-2 * span // TILE) * TILE
    args = (
        factor, load, dof_map, dof_sign, live_count, face_slot, face_count, node_coord.transpose(0, 2, 1, 3), coarse_inverse
    )
    shape = jax.ShapeDtypeStruct
    turns = ITERS + 2
    multipliers, projected = pl.pallas_call(
        functools.partial(pcg_kernel, groups, members),
        name="pcg",
        out_shape=(shape((subs, size), F32), shape((subs, size), F32)),
        in_specs=[pl.BlockSpec(memory_space=pltpu.HBM)] * len(args),
        out_specs=[pl.BlockSpec(memory_space=pltpu.VMEM)] * 2,
        scratch_shapes=[pltpu.VMEM(value.shape, value.dtype) for value in args]
        + [
            pltpu.VMEM((subs, size, size), F32),
            pltpu.VMEM((subs, size, faces), BF16),
            pltpu.VMEM((subs, size, faces), BF16),
            pltpu.VMEM((subs, size, size), BF16),
            pltpu.VMEM((subs, size), F32),
            pltpu.VMEM((subs, size), F32),
            pltpu.VMEM((subs, 8, size), F32),
            pltpu.VMEM((subs, 8, faces), F32),
            pltpu.VMEM((subs, 8, TILE), F32),
            pltpu.VMEM((subs, members, 8, width), F32),
            pltpu.SemaphoreType.DMA((len(args),)),
            pltpu.VMEM((5, subs, members, 8, width), F32),
            pltpu.VMEM((4, subs, 8, faces), F32),
            pltpu.VMEM((subs, 40, size), F32),
            pltpu.VMEM((turns, groups * members, 1, message), F32),
            pltpu.VMEM((turns, 1, message), F32),
            pltpu.VMEM((turns - 1, 4, subs, 1, faces), F32),
            pltpu.VMEM((turns - 1, subs, 1, faces), F32),
            pltpu.SemaphoreType.DMA((turns,)),
            pltpu.SemaphoreType.DMA((turns,)),
            pltpu.SemaphoreType.DMA((turns - 1, 4)),
            pltpu.SemaphoreType.DMA((turns - 1, 4)),
            pltpu.SemaphoreType.DMA((2, 4)),
            pltpu.SemaphoreType.DMA((2, 4)),
        ],
        compiler_params=pltpu.CompilerParams(
            collective_id=0, has_side_effects=True, vmem_limit_bytes=VMEM_LIMIT
        ),
    )(*args)
    return multipliers[None], projected[None]


def solution(mesh):
    return jax.shard_map(
        functools.partial(shards, mesh.shape["group"], mesh.shape["member"]),
        mesh=mesh,
        in_specs=(
            P("group", "member", None, None),
            P("group", "member", None),
            P("group", "member", None),
            P("group", "member", None),
            P("group", "member"),
            P("group", "member", None, None),
            P("group", "member", None),
            P("group", "member", None, None),
            P(("group", "member"), None),
        ),
        out_specs=(P("group", "member", None), P("group", "member", None)),
        check_vma=False,
    )
```

```python
import functools

import jax
import jax.numpy as jnp
from jax import lax
from jax.experimental import pallas as pl
from jax.experimental.pallas import tpu as pltpu
from jax.sharding import PartitionSpec as P

ITERS = 3
BASE = 16
TILE = 128
HALF_SPAN = 8.0
VMEM_LIMIT = 62 * 2**20
LEFT, RIGHT, DOWN, UP = range(4)
F32 = jnp.float32
BF16 = jnp.bfloat16
NT = (((1,), (1,)), ((), ()))
NN = (((1,), (0,)), ((), ()))


def iota(shape, dim):
    return lax.broadcasted_iota(jnp.int32, shape, dim)


def dot(left, right, dims=NN):
    return lax.dot_general(left, right, dims, preferred_element_type=F32)


def parts_of(values, count):
    parts = []
    for _ in range(count):
        part = values.astype(BF16)
        parts.append(part)
        values = values - part.astype(F32)
    return parts


def mm(left, right):
    left_hi, left_lo = parts_of(left, 2)
    right_hi, right_lo = parts_of(right, 2)
    return dot(left_hi, right_hi) + (dot(left_hi, right_lo) + dot(left_lo, right_hi))


def row_times(rows, table, dims=NN):
    stacked = []
    for row in rows:
        for part in parts_of(row, 3):
            stacked.append(part.astype(F32))
    pad = -len(stacked) % 8
    stacked.append(jnp.zeros((pad, rows[0].shape[1]), F32))
    product = dot(jnp.concatenate(stacked, axis=0).astype(BF16), table, dims)
    return [
        product[3 * at : 3 * at + 1] + product[3 * at + 1 : 3 * at + 2] + product[3 * at + 2 : 3 * at + 3]
        for at in range(len(rows))
    ]


def invert(factor, linv, subs):
    size = factor.shape[1]
    blocks = size // TILE
    row = iota((TILE, TILE), 0)
    lane = iota((TILE, TILE), 1)
    shift = BASE.bit_length() - 1
    same = (row >> shift) == (lane >> shift)
    where_at = [(s, b) for s in range(subs) for b in range(blocks)]

    def diagonal(s, b):
        return factor[s, b * TILE : (b + 1) * TILE, b * TILE : (b + 1) * TILE]

    packed = []
    for s, b in where_at:
        kept = jnp.where(same, diagonal(s, b), 0.0)
        packed.append(jnp.sum(kept.reshape(TILE // BASE, BASE, TILE), axis=0))
    count = len(packed)
    packed = jnp.concatenate(packed, axis=0)
    wide = (TILE, BASE * TILE)
    source, target = iota(wide, 0), iota(wide, 1)
    spread = (((source & (BASE - 1)) == (target >> 7)) & ((source >> shift) == ((target & 127) >> shift)))
    spread = jnp.where(spread, 1.0, 0.0).astype(BF16)
    columns = sum(dot(part, spread) for part in parts_of(packed, 3))
    within = iota((count, BASE, TILE), 1)
    solved = jnp.where(within == (iota((count, BASE, TILE), 2) & (BASE - 1)), 1.0, 0.0)
    for m in range(BASE):
        column = columns[:, m * TILE : (m + 1) * TILE].reshape(count, BASE, TILE)
        pivot = solved[:, m : m + 1, :] / column[:, m : m + 1, :]
        solved = jnp.where(within > m, solved - column * pivot, jnp.where(within == m, pivot, solved))
    inverses = [
        jnp.where(same, jnp.concatenate([solved[at]] * (TILE // BASE), axis=0), 0.0) for at in range(count)
    ]
    width = BASE
    while width < TILE:
        level = width.bit_length() - 1
        below = (
            ((row >> (level + 1)) == (lane >> (level + 1)))
            & (((row >> level) & 1) == 1)
            & (((lane >> level) & 1) == 0)
        )
        middle = [
            mm(jnp.where(below, diagonal(s, b), 0.0), inverses[at]) for at, (s, b) in enumerate(where_at)
        ]
        inverses = [inverses[at] - mm(inverses[at], middle[at]) for at in range(count)]
        width *= 2
    for at, (s, b) in enumerate(where_at):
        rows = slice(b * TILE, (b + 1) * TILE)
        linv[s, rows, rows] = inverses[at]
        if b + 1 < blocks:
            linv[s, rows, (b + 1) * TILE :] = jnp.zeros((TILE, size - (b + 1) * TILE), F32)
    width = TILE
    while width < size:
        for start in range(0, size - width, 2 * width):
            middle_at, end = start + width, min(start + 2 * width, size)
            for s in range(subs):
                upper = linv[s, start:middle_at, start:middle_at]
                lower = linv[s, middle_at:end, middle_at:end]
                linv[s, middle_at:end, start:middle_at] = -mm(lower, mm(factor[s, middle_at:end, start:middle_at], upper))
        width *= 2


def tables(
    live, face_count, load, dof_map, dof_sign, face_slot, coord,
    pack, unpack, slots, mask, weight, modes, face_modes, rhs,
):
    subs, size = load.shape
    cap = face_slot.shape[2]
    nodes = coord.shape[2]
    for s in range(subs):
        sign_row = jnp.where(iota((1, size), 1) < live[0:1, s : s + 1], dof_sign[s : s + 1, :].astype(F32), 0.0)
        slot_rows = jnp.where(iota((size, size), 0) == dof_map[s : s + 1, :], sign_row, 0.0).astype(BF16)
        slots[s] = slot_rows

        def table_of(order):
            face_row = jnp.concatenate([face_slot[s, f : f + 1, :] for f in order], axis=1)
            lane = iota((1, 4 * cap), 1)
            limit = jnp.zeros((1, 4 * cap), jnp.int32)
            for at, f in enumerate(order):
                limit = jnp.where(lane // cap == at, at * cap + face_count[s : s + 1, f : f + 1], limit)
            face_row = jnp.where(lane < limit, face_row, -1)
            hit = jnp.where(iota((size, 4 * cap), 0) == face_row, 1.0, 0.0).astype(BF16)
            return dot(slot_rows, hit).astype(BF16)

        outgoing = table_of((0, 1, 2, 3))
        pack[s] = outgoing
        unpack[s] = table_of((1, 0, 3, 2))
        live_row = jnp.abs(dot(jnp.ones((8, size), BF16), slot_rows, NT))[0:1]
        shared = dot(jnp.ones((8, 4 * cap), BF16), jnp.abs(outgoing), NT)[0:1]
        mask[s : s + 1, :] = live_row
        weight[s : s + 1, :] = live_row * (1.0 - 0.5 * shared)
        position = jnp.concatenate([coord[axis, s : s + 1, :] for axis in range(3)], axis=0)
        position = (position.astype(F32) - HALF_SPAN) / HALF_SPAN
        stacked = jnp.concatenate(
            [position, iota((1, nodes), 1).astype(F32), jnp.zeros((4, nodes), F32)], axis=0
        ).astype(BF16)
        first_of = 3 * iota((nodes, size), 0)
        unknown = iota((nodes, size), 1)
        of_node = jnp.where((unknown >= first_of) & (unknown < first_of + 3), 1.0, 0.0).astype(BF16)
        spread = dot(stacked, of_node)
        x, y, z = spread[0:1], spread[1:2], spread[2:3]
        component = iota((1, size), 1).astype(F32) - 3.0 * spread[3:4]
        first = jnp.where(component == 0.0, 1.0, 0.0)
        second = jnp.where(component == 1.0, 1.0, 0.0)
        third = jnp.where(component == 2.0, 1.0, 0.0)
        table = jnp.concatenate(
            [
                first,
                second,
                third,
                third * y - second * z,
                first * z - third * x,
                second * x - first * y,
                jnp.zeros((2, size), F32),
            ],
            axis=0,
        )
        modes[s] = table * live_row
        face_modes[s] = dot(table.astype(BF16), outgoing)
        rhs[s] = jnp.broadcast_to(jnp.sum(table * load[s : s + 1, :], axis=1, keepdims=True), (8, TILE))


def coarse_layout(raw, coarse, groups, members):
    width = coarse.shape[-1]
    none = jnp.zeros((2, raw.shape[1]), F32)
    rows = jnp.concatenate([raw[0:6, :], none, raw[6:12, :], none], axis=0)
    stacked = jnp.concatenate([part.astype(F32) for part in parts_of(rows, 3)], axis=0).astype(BF16)

    def one(at, carry):
        lane = iota((1, width), 1)
        column = 12 * ((lane >> 4) * members + at) + 6 * ((lane >> 3) & 1) + (lane & 7)
        column = jnp.where(((lane & 7) < 6) & (lane < 16 * groups), column, -1)
        pick = jnp.where(iota((raw.shape[1], width), 0) == column, 1.0, 0.0).astype(BF16)
        picked = dot(stacked, pick)
        picked = picked[0:16] + picked[16:32] + picked[32:48]
        coarse[0, at] = picked[0:8]
        coarse[1, at] = picked[8:16]
        return carry

    lax.fori_loop(0, members, one, 0, unroll=members <= 8)


def pcg_kernel(
    groups, members,
    factor_hbm, load_hbm, dof_map_hbm, dof_sign_hbm, live_hbm, face_slot_hbm, face_count_hbm, coord_hbm, raw_hbm,
    out,
    factor_own, load_own, dof_map_own, dof_sign_own, live_own, face_slot_own, face_count_own, coord_own, raw_own,
    linv, pack, unpack, slots, mask, weight, modes, face_modes, rhs, coarse, load_sem,
    inverse_rows, face_in, shape_rows, across_in, across_out, along_in, along_out, halo_in, halo_out,
    send_across, recv_across, send_along, recv_along, send_halo, recv_halo, send_setup, recv_setup,
):
    loads = [
        pltpu.make_async_copy(src, dst, load_sem.at[at])
        for at, (src, dst) in enumerate((
            (load_hbm, load_own), (dof_map_hbm, dof_map_own), (dof_sign_hbm, dof_sign_own),
            (live_hbm, live_own), (face_slot_hbm, face_slot_own), (face_count_hbm, face_count_own),
            (coord_hbm, coord_own), (raw_hbm, raw_own), (factor_hbm, factor_own),
        ))
    ]
    for copy in loads:
        copy.start()
    factor, load = factor_own.at[0], load_own.at[0]
    subs, size = load.shape
    faces = pack.shape[2]
    cap = faces // 4
    span = 16 * groups
    width = coarse.shape[-1]
    message = across_out.shape[-1]
    c, m = lax.axis_index("group"), lax.axis_index("member")
    neighbours = (
        (m > 0, (c, lax.rem(m + members - 1, members))),
        (m < members - 1, (c, lax.rem(m + 1, members))),
        (c > 0, (lax.rem(c + groups - 1, groups), m)),
        (c < groups - 1, (lax.rem(c + 1, groups), m)),
    )
    opposite = (RIGHT, LEFT, UP, DOWN)

    across = [lax.rem(c + step, groups) for step in range(groups)]
    along = [lax.rem(m + step, members) for step in range(members)]

    def each_across(action):
        for off in range(groups - 1, 0, -1):
            action((across[off], m))

    def each_along(action):
        for far in range(members - 1, 0, -1):
            action((c, along[far]))

    inverse_rows[...] = jnp.zeros(inverse_rows.shape, F32)
    face_in[...] = jnp.zeros(face_in.shape, F32)
    halo_in[...] = jnp.zeros(halo_in.shape, F32)

    barrier = pltpu.get_barrier_semaphore()

    def greet(where):
        pl.semaphore_signal(barrier, inc=1, device_id=where, device_id_type=pl.DeviceIdType.MESH)

    each_across(greet)
    each_along(greet)
    for copy in loads[:-1]:
        copy.wait()
    tables(
        live_own, face_count_own.at[0], load, dof_map_own.at[0], dof_sign_own.at[0], face_slot_own.at[0],
        coord_own.at[0], pack, unpack, slots, mask, weight, modes, face_modes, rhs,
    )
    coarse_layout(raw_own, coarse, groups, members)
    pl.semaphore_wait(barrier, groups + members - 2)

    def remote(src, dst, send, recv, where):
        return pltpu.make_async_remote_copy(
            src_ref=src, dst_ref=dst, send_sem=send, recv_sem=recv,
            device_id=where, device_id_type=pl.DeviceIdType.MESH,
        )

    def sided(ref, way):
        if way == LEFT:
            return ref.at[0]
        return ref.at[1] if way == RIGHT else ref

    def halo_copy(turn, way):
        to = opposite[way]
        return remote(
            sided(halo_out.at[turn], way), sided(halo_in.at[turn, to], way),
            send_halo.at[turn, way], recv_halo.at[turn, to], neighbours[way][1],
        )

    def face_copy(way):
        to = opposite[way]
        return remote(
            sided(face_modes, way), sided(face_in.at[to], way),
            send_setup.at[0, way], recv_setup.at[0, to], neighbours[way][1],
        )

    def coarse_copy(way):
        to = opposite[way]
        return remote(
            sided(coarse, way),
            (inverse_rows.at[2, 1], inverse_rows.at[1, 0], inverse_rows.at[4], inverse_rows.at[3])[way],
            send_setup.at[1, way], recv_setup.at[1, to], neighbours[way][1],
        )

    def each_way(action):
        for way in range(4):
            @pl.when(neighbours[way][0])
            def _():
                action(way)

    def across_view(turn):
        return across_in.at[turn, pl.ds(0, groups - 1)]

    def along_view(turn):
        return along_in.at[turn, pl.ds(0, members - 1)]

    def wait_all(view, sem):
        pltpu.make_async_copy(view, view, sem).wait()

    def gather_start(turn, row):
        across_out[turn] = row
        across_in[turn, c] = row
        each_across(
            lambda where: remote(
                across_out.at[turn], across_in.at[turn, c], send_across.at[turn], recv_across.at[turn], where
            ).start()
        )

    def gather_middle(turn):
        wait_all(across_view(turn), recv_across.at[turn])
        row = jnp.sum(across_in[turn], axis=0)
        along_out[turn] = row
        along_in[turn, m] = row
        each_along(
            lambda where: remote(
                along_out.at[turn], along_in.at[turn, m], send_along.at[turn], recv_along.at[turn], where
            ).start()
        )

    def gather_wait(turn):
        wait_all(along_view(turn), recv_along.at[turn])

    lane_row = iota((1, message), 1)

    def placing(s):
        at = iota((40, message), 0)
        lane = iota((40, message), 1)
        kind, a = at >> 3, at & 7
        own = 16 * c + 8 * s
        to_left = own - 8 if s == 1 else span + 16 * c + 8
        to_right = own + 8 if s == 0 else span + 16 * c
        base = jnp.where(kind == 0, own, jnp.where(kind == 1, to_left, jnp.where(
            kind == 2, to_right, jnp.where(kind == 3, own - 16, own + 16))))
        return jnp.where((lane == base + a) & (a < 6), 1.0, 0.0)

    places = [placing(s) for s in range(subs)]

    def coarse_sum(turn):
        summed = along_in[turn].reshape(members, message)
        if span >= TILE:
            low, high = summed[:, :span], summed[:, span : 2 * span]
        else:
            lane = iota((members, message), 1)
            low = jnp.where(lane < span, summed, 0.0)
            high = jnp.where(lane < span, pltpu.roll(summed, message - span, 1), 0.0)
        second = ((iota((members, width), 1) >> 3) & 1) == 1
        none = jnp.zeros((1, width), F32)
        from_right = jnp.concatenate([high[1:], none], axis=0)
        from_left = jnp.concatenate([none, high[:-1]], axis=0)
        return low + jnp.where(second, from_right, from_left)

    def correction(coarse_values):
        fields = []
        for s in range(subs):
            spread = jnp.zeros((8, size), F32)
            for kind in range(5):
                product = jnp.zeros((8, width), F32)
                for at in range(members):
                    product = product + inverse_rows[kind, s, at] * coarse_values[at : at + 1, :]
                alpha = jnp.sum(product, axis=1, keepdims=True)
                spread = spread + shape_rows[s, 8 * kind : 8 * kind + 8, :] * alpha
            fields.append(jnp.sum(spread, axis=0, keepdims=True))
        return fields

    def apply_dual(fields):
        images = []
        for s in range(subs):
            sums = [jnp.zeros((8, TILE), F32) for _ in range(size // TILE)]
            for b in range(size // TILE):
                reach = (b + 1) * TILE
                panel = linv[s, b * TILE : reach, :reach]
                column = jnp.sum(panel * fields[s][:, :reach], axis=1, keepdims=True)
                for at in range(b + 1):
                    piece = panel[:, at * TILE : (at + 1) * TILE] * column
                    sums[at] = sums[at] + jnp.sum(piece.reshape(TILE // 8, 8, TILE), axis=0)
            image = jnp.concatenate([jnp.sum(part, axis=0, keepdims=True) for part in sums], axis=1)
            images.append(image * mask[s : s + 1, :])
        return images

    face_lane = iota((1, faces), 1)

    def from_faces(right, left, up, down):
        return jnp.where(
            face_lane < cap, right,
            jnp.where(face_lane < 2 * cap, left, jnp.where(face_lane < 3 * cap, up, down)),
        )

    def project(turn, fields, scalars):
        outgoing = [row_times([fields[s]], pack[s])[0] for s in range(subs)]
        for s in range(subs):
            halo_out[turn - 1, s] = outgoing[s]
        each_way(lambda way: halo_copy(turn - 1, way).start())
        row = jnp.zeros((1, message), F32)
        for s in range(subs):
            column = jnp.sum(shape_rows[s] * fields[s], axis=1, keepdims=True)
            row = row + jnp.sum(places[s] * column, axis=0, keepdims=True)
        spare = (6, 7, 14)
        for at, value in enumerate(scalars):
            row = row + jnp.where(lane_row == 16 * c + spare[at], value, 0.0)
        gather_start(turn, row)
        gather_middle(turn)
        each_way(lambda way: halo_copy(turn - 1, opposite[way]).wait_recv())
        arrived = halo_in.at[turn - 1]
        rights = (outgoing[1], arrived[RIGHT, 0])
        lefts = (arrived[LEFT, 1], outgoing[0])
        assembled = []
        for s in range(subs):
            incoming = from_faces(rights[s], lefts[s], arrived[UP, s], arrived[DOWN, s])
            assembled.append(fields[s] + row_times([incoming], unpack[s], NT)[0])
        gather_wait(turn)
        values = coarse_sum(turn)
        fixes = correction(values)
        spare_lane = iota(values.shape, 1) & 15
        sums = []
        for at in range(len(scalars)):
            kept = jnp.where(spare_lane == spare[at], values, 0.0)
            sums.append(jnp.sum(jnp.sum(kept, axis=1, keepdims=True), axis=0, keepdims=True))
        return [assembled[s] - fixes[s] for s in range(subs)], sums

    each_way(lambda way: face_copy(way).start())
    each_way(lambda way: coarse_copy(way).start())
    row = jnp.zeros((1, message), F32)
    for s in range(subs):
        column = jnp.concatenate([rhs[s][:, 0:1], jnp.zeros((32, 1), F32)], axis=0)
        row = row + jnp.sum(places[s] * column, axis=0, keepdims=True)
    gather_start(0, row)
    for s in range(subs):
        inverse_rows[0, s] = coarse[s]
    inverse_rows[2, 0] = coarse[1]
    inverse_rows[1, 1] = coarse[0]
    loads[-1].wait()
    gather_middle(0)
    invert(factor, linv, subs)
    each_way(lambda way: face_copy(opposite[way]).wait_recv())
    each_way(lambda way: coarse_copy(opposite[way]).wait_recv())
    rights = (face_modes[1], face_in[RIGHT, 0])
    lefts = (face_in[LEFT, 1], face_modes[0])
    block = iota((8, faces), 1) // cap
    for s in range(subs):
        sources = (lefts[s], rights[s], face_in[DOWN, s], face_in[UP, s])
        spread = jnp.concatenate(
            [jnp.where(block == (1, 0, 3, 2)[f], sources[f], 0.0) for f in range(4)], axis=0
        ).astype(BF16)
        shape_rows[s, 0:8, :] = modes[s]
        shape_rows[s, 8:40, :] = dot(spread, unpack[s], NT)
    gather_wait(0)
    multipliers = correction(coarse_sum(0))
    start = apply_dual([load[s : s + 1, :] - multipliers[s] for s in range(subs)])
    projected, _ = project(1, start, [])
    for turn in range(ITERS):
        image = apply_dual(projected)
        norm = sum(
            jnp.sum(weight[s : s + 1, :] * projected[s] * projected[s], axis=1, keepdims=True) for s in range(subs)
        )
        energy = sum(jnp.sum(projected[s] * image[s], axis=1, keepdims=True) for s in range(subs))
        partials = [norm, energy]
        if turn:
            partials.append(
                sum(jnp.sum(projected[s] * direction_image[s], axis=1, keepdims=True) for s in range(subs))
            )
        change, sums = project(2 + turn, image, partials)
        if turn:
            ratio = sums[0] / norm_now
            curvature = sums[1] + 2.0 * ratio * sums[2] + ratio * ratio * curvature
            direction = [projected[s] + ratio * direction[s] for s in range(subs)]
            direction_image = [image[s] + ratio * direction_image[s] for s in range(subs)]
            direction_change = [change[s] + ratio * direction_change[s] for s in range(subs)]
        else:
            curvature = sums[1]
            direction, direction_image, direction_change = projected, image, change
        norm_now = sums[0]
        step = norm_now / curvature
        multipliers = [multipliers[s] + step * direction[s] for s in range(subs)]
        projected = [projected[s] - step * direction_change[s] for s in range(subs)]
    for s in range(subs):
        ordered = row_times([multipliers[s], projected[s]], slots[s])
        out[0, s : s + 1, :] = ordered[0]
        out[1, s : s + 1, :] = ordered[1]

    each_way(lambda way: face_copy(way).wait_send())
    each_way(lambda way: coarse_copy(way).wait_send())
    for turn in range(ITERS + 1):
        each_way(lambda way: halo_copy(turn, way).wait_send())
    for turn in range(ITERS + 2):
        wait_all(across_view(turn), send_across.at[turn])
        wait_all(along_view(turn), send_along.at[turn])


def shards(
    groups, members,
    factor, load, dof_map, dof_sign, live_count, face_slot, face_count, node_coord, coarse_inverse,
):
    subs, size = load.shape[1:]
    faces = 4 * face_slot.shape[3]
    span = 16 * groups
    width = -(-span // TILE) * TILE
    message = -(-2 * span // TILE) * TILE
    args = (
        factor, load, dof_map, dof_sign, live_count, face_slot, face_count, node_coord.transpose(0, 2, 1, 3), coarse_inverse
    )
    shape = jax.ShapeDtypeStruct
    turns = ITERS + 2
    result = pl.pallas_call(
        functools.partial(pcg_kernel, groups, members),
        name="pcg",
        out_shape=shape((2, subs, size), F32),
        in_specs=[pl.BlockSpec(memory_space=pltpu.HBM)] * len(args),
        out_specs=pl.BlockSpec(memory_space=pltpu.VMEM),
        scratch_shapes=[pltpu.VMEM(value.shape, value.dtype) for value in args]
        + [
            pltpu.VMEM((subs, size, size), F32),
            pltpu.VMEM((subs, size, faces), BF16),
            pltpu.VMEM((subs, size, faces), BF16),
            pltpu.VMEM((subs, size, size), BF16),
            pltpu.VMEM((subs, size), F32),
            pltpu.VMEM((subs, size), F32),
            pltpu.VMEM((subs, 8, size), F32),
            pltpu.VMEM((subs, 8, faces), F32),
            pltpu.VMEM((subs, 8, TILE), F32),
            pltpu.VMEM((subs, members, 8, width), F32),
            pltpu.SemaphoreType.DMA((len(args),)),
            pltpu.VMEM((5, subs, members, 8, width), F32),
            pltpu.VMEM((4, subs, 8, faces), F32),
            pltpu.VMEM((subs, 40, size), F32),
            pltpu.VMEM((turns, groups, 1, message), F32),
            pltpu.VMEM((turns, 1, message), F32),
            pltpu.VMEM((turns, members, 1, message), F32),
            pltpu.VMEM((turns, 1, message), F32),
            pltpu.VMEM((turns - 1, 4, subs, 1, faces), F32),
            pltpu.VMEM((turns - 1, subs, 1, faces), F32),
            pltpu.SemaphoreType.DMA((turns,)),
            pltpu.SemaphoreType.DMA((turns,)),
            pltpu.SemaphoreType.DMA((turns,)),
            pltpu.SemaphoreType.DMA((turns,)),
            pltpu.SemaphoreType.DMA((turns - 1, 4)),
            pltpu.SemaphoreType.DMA((turns - 1, 4)),
            pltpu.SemaphoreType.DMA((2, 4)),
            pltpu.SemaphoreType.DMA((2, 4)),
        ],
        compiler_params=pltpu.CompilerParams(
            collective_id=0, has_side_effects=True, vmem_limit_bytes=VMEM_LIMIT
        ),
    )(*args)
    return result[0:1], result[1:2]


def solution(mesh):
    return jax.shard_map(
        functools.partial(shards, mesh.shape["group"], mesh.shape["member"]),
        mesh=mesh,
        in_specs=(
            P("group", "member", None, None),
            P("group", "member", None),
            P("group", "member", None),
            P("group", "member", None),
            P("group", "member"),
            P("group", "member", None, None),
            P("group", "member", None),
            P("group", "member", None, None),
            P(("group", "member"), None),
        ),
        out_specs=(P("group", "member", None), P("group", "member", None)),
        check_vma=False,
    )
```

```python
import functools

import jax
import jax.numpy as jnp
from jax import lax
from jax.experimental import pallas as pl
from jax.experimental.pallas import tpu as pltpu
from jax.sharding import PartitionSpec as P

ITERS = 3
BASE = 16
TILE = 128
HALF_SPAN = 8.0
VMEM_LIMIT = 62 * 2**20
LEFT, RIGHT, DOWN, UP = range(4)
F32 = jnp.float32
BF16 = jnp.bfloat16
NT = (((1,), (1,)), ((), ()))
NN = (((1,), (0,)), ((), ()))


def iota(shape, dim):
    return lax.broadcasted_iota(jnp.int32, shape, dim)


def dot(left, right, dims=NN):
    return lax.dot_general(left, right, dims, preferred_element_type=F32)


def parts_of(values, count):
    parts = []
    for _ in range(count):
        part = values.astype(BF16)
        parts.append(part)
        values = values - part.astype(F32)
    return parts


def mm(left, right):
    left_hi, left_lo = parts_of(left, 2)
    right_hi, right_lo = parts_of(right, 2)
    if left.shape[1] == TILE:
        deep = dot(
            jnp.concatenate([left_hi, left_lo], axis=1), jnp.concatenate([right_hi, right_hi], axis=0)
        )
        return deep + dot(left_hi, right_lo)
    return dot(left_hi, right_hi) + (dot(left_hi, right_lo) + dot(left_lo, right_hi))


def row_times(rows, table, dims=NN):
    stacked = []
    for row in rows:
        for part in parts_of(row, 3):
            stacked.append(part.astype(F32))
    pad = -len(stacked) % 8
    stacked.append(jnp.zeros((pad, rows[0].shape[1]), F32))
    product = dot(jnp.concatenate(stacked, axis=0).astype(BF16), table, dims)
    return [
        product[3 * at : 3 * at + 1] + product[3 * at + 1 : 3 * at + 2] + product[3 * at + 2 : 3 * at + 3]
        for at in range(len(rows))
    ]


def invert(factor, linv, subs):
    size = factor.shape[1]
    blocks = size // TILE
    row = iota((TILE, TILE), 0)
    lane = iota((TILE, TILE), 1)
    shift = BASE.bit_length() - 1
    same = (row >> shift) == (lane >> shift)
    where_at = [(s, b) for s in range(subs) for b in range(blocks)]

    def diagonal(s, b):
        return factor[s, b * TILE : (b + 1) * TILE, b * TILE : (b + 1) * TILE]

    packed = []
    for s, b in where_at:
        kept = jnp.where(same, diagonal(s, b), 0.0)
        packed.append(jnp.sum(kept.reshape(TILE // BASE, BASE, TILE), axis=0))
    count = len(packed)
    packed = jnp.concatenate(packed, axis=0)
    wide = (TILE, BASE * TILE)
    source, target = iota(wide, 0), iota(wide, 1)
    spread = (((source & (BASE - 1)) == (target >> 7)) & ((source >> shift) == ((target & 127) >> shift)))
    spread = jnp.where(spread, 1.0, 0.0).astype(BF16)
    high, middle, low = parts_of(packed, 3)
    columns = dot(
        jnp.concatenate([high, middle], axis=1), jnp.concatenate([spread, spread], axis=0)
    ) + dot(low, spread)
    within = iota((count, BASE, TILE), 1)
    solved = jnp.where(within == (iota((count, BASE, TILE), 2) & (BASE - 1)), 1.0, 0.0)
    for m in range(BASE):
        column = columns[:, m * TILE : (m + 1) * TILE].reshape(count, BASE, TILE)
        pivot = solved[:, m : m + 1, :] / column[:, m : m + 1, :]
        solved = jnp.where(within > m, solved - column * pivot, jnp.where(within == m, pivot, solved))
    inverses = [
        jnp.where(same, jnp.concatenate([solved[at]] * (TILE // BASE), axis=0), 0.0) for at in range(count)
    ]
    width = BASE
    while width < TILE:
        level = width.bit_length() - 1
        below = (
            ((row >> (level + 1)) == (lane >> (level + 1)))
            & (((row >> level) & 1) == 1)
            & (((lane >> level) & 1) == 0)
        )
        middle = [
            mm(jnp.where(below, diagonal(s, b), 0.0), inverses[at]) for at, (s, b) in enumerate(where_at)
        ]
        inverses = [inverses[at] - mm(inverses[at], middle[at]) for at in range(count)]
        width *= 2
    for at, (s, b) in enumerate(where_at):
        rows = slice(b * TILE, (b + 1) * TILE)
        linv[s, rows, rows] = inverses[at]
        if b + 1 < blocks:
            linv[s, rows, (b + 1) * TILE :] = jnp.zeros((TILE, size - (b + 1) * TILE), F32)
    width = TILE
    while width < size:
        for start in range(0, size - width, 2 * width):
            middle_at, end = start + width, min(start + 2 * width, size)
            for s in range(subs):
                upper = linv[s, start:middle_at, start:middle_at]
                lower = linv[s, middle_at:end, middle_at:end]
                linv[s, middle_at:end, start:middle_at] = -mm(lower, mm(factor[s, middle_at:end, start:middle_at], upper))
        width *= 2


def tables(
    live, face_count, load, dof_map, dof_sign, face_slot, coord,
    pack, unpack, slots, mask, weight, modes, face_modes, rhs,
):
    subs, size = load.shape
    cap = face_slot.shape[2]
    nodes = coord.shape[2]
    for s in range(subs):
        sign_row = jnp.where(iota((1, size), 1) < live[0:1, s : s + 1], dof_sign[s : s + 1, :].astype(F32), 0.0)
        slot_rows = jnp.where(iota((size, size), 0) == dof_map[s : s + 1, :], sign_row, 0.0).astype(BF16)
        slots[s] = slot_rows

        def table_of(order):
            face_row = jnp.concatenate([face_slot[s, f : f + 1, :] for f in order], axis=1)
            lane = iota((1, 4 * cap), 1)
            limit = jnp.zeros((1, 4 * cap), jnp.int32)
            for at, f in enumerate(order):
                limit = jnp.where(lane // cap == at, at * cap + face_count[s : s + 1, f : f + 1], limit)
            face_row = jnp.where(lane < limit, face_row, -1)
            hit = jnp.where(iota((size, 4 * cap), 0) == face_row, 1.0, 0.0).astype(BF16)
            return dot(slot_rows, hit)

        outgoing = table_of((0, 1, 2, 3)).astype(BF16)
        pack[s] = outgoing
        unpack[s] = table_of((1, 0, 3, 2)).T.astype(BF16)
        live_row = jnp.abs(dot(jnp.ones((8, size), BF16), slot_rows, NT))[0:1]
        shared = dot(jnp.ones((8, 4 * cap), BF16), jnp.abs(outgoing), NT)[0:1]
        mask[s : s + 1, :] = live_row
        weight[s : s + 1, :] = live_row * (1.0 - 0.5 * shared)
        position = jnp.concatenate([coord[axis, s : s + 1, :] for axis in range(3)], axis=0)
        position = (position.astype(F32) - HALF_SPAN) / HALF_SPAN
        stacked = jnp.concatenate(
            [position, iota((1, nodes), 1).astype(F32), jnp.zeros((4, nodes), F32)], axis=0
        ).astype(BF16)
        first_of = 3 * iota((nodes, size), 0)
        unknown = iota((nodes, size), 1)
        of_node = jnp.where((unknown >= first_of) & (unknown < first_of + 3), 1.0, 0.0).astype(BF16)
        spread = dot(stacked, of_node)
        x, y, z = spread[0:1], spread[1:2], spread[2:3]
        component = iota((1, size), 1).astype(F32) - 3.0 * spread[3:4]
        first = jnp.where(component == 0.0, 1.0, 0.0)
        second = jnp.where(component == 1.0, 1.0, 0.0)
        third = jnp.where(component == 2.0, 1.0, 0.0)
        table = jnp.concatenate(
            [
                first,
                second,
                third,
                third * y - second * z,
                first * z - third * x,
                second * x - first * y,
                jnp.zeros((2, size), F32),
            ],
            axis=0,
        )
        modes[s] = table * live_row
        face_modes[s] = dot(table.astype(BF16), outgoing)
        rhs[s] = jnp.broadcast_to(jnp.sum(table * load[s : s + 1, :], axis=1, keepdims=True), (8, TILE))


def coarse_layout(raw, coarse, groups, members):
    width = coarse.shape[-1]
    none = jnp.zeros((2, raw.shape[1]), F32)
    rows = jnp.concatenate([raw[0:6, :], none, raw[6:12, :], none], axis=0)
    stacked = jnp.concatenate([part.astype(F32) for part in parts_of(rows, 3)], axis=0).astype(BF16)

    def one(at, carry):
        lane = iota((1, width), 1)
        column = 12 * ((lane >> 4) * members + at) + 6 * ((lane >> 3) & 1) + (lane & 7)
        column = jnp.where(((lane & 7) < 6) & (lane < 16 * groups), column, -1)
        pick = jnp.where(iota((raw.shape[1], width), 0) == column, 1.0, 0.0).astype(BF16)
        picked = dot(stacked, pick)
        picked = picked[0:16] + picked[16:32] + picked[32:48]
        coarse[0, at] = picked[0:8]
        coarse[1, at] = picked[8:16]
        return carry

    lax.fori_loop(0, members, one, 0, unroll=members <= 8)


def pcg_kernel(
    groups, members,
    factor_hbm, load_hbm, dof_map_hbm, dof_sign_hbm, live_hbm, face_slot_hbm, face_count_hbm, coord_hbm, raw_hbm,
    out,
    factor_own, load_own, dof_map_own, dof_sign_own, live_own, face_slot_own, face_count_own, coord_own, raw_own,
    linv, pack, unpack, slots, mask, weight, modes, face_modes, rhs, coarse, load_sem,
    inverse_rows, face_in, shape_rows, gather_in, gather_out, halo_in, halo_out,
    send_gather, recv_gather, send_halo, recv_halo, send_setup, recv_setup,
):
    loads = [
        pltpu.make_async_copy(src, dst, load_sem.at[at])
        for at, (src, dst) in enumerate((
            (load_hbm, load_own), (dof_map_hbm, dof_map_own), (dof_sign_hbm, dof_sign_own),
            (live_hbm, live_own), (face_slot_hbm, face_slot_own), (face_count_hbm, face_count_own),
            (coord_hbm, coord_own), (raw_hbm, raw_own), (factor_hbm, factor_own),
        ))
    ]
    for copy in loads:
        copy.start()
    factor, load = factor_own.at[0], load_own.at[0]
    subs, size = load.shape
    faces = pack.shape[2]
    cap = faces // 4
    total = groups * members
    span = 16 * groups
    width = coarse.shape[-1]
    message = gather_out.shape[-1]
    c, m = lax.axis_index("group"), lax.axis_index("member")
    me = c * members + m
    neighbours = (
        (m > 0, (c, lax.rem(m + members - 1, members))),
        (m < members - 1, (c, lax.rem(m + 1, members))),
        (c > 0, (lax.rem(c + groups - 1, groups), m)),
        (c < groups - 1, (lax.rem(c + 1, groups), m)),
    )
    opposite = (RIGHT, LEFT, UP, DOWN)

    across = [lax.rem(c + step, groups) for step in range(groups)]
    along = [lax.rem(m + step, members) for step in range(members)]

    def each_peer(action):
        if total <= 32:
            for far in range(members - 1, -1, -1):
                for off in range(groups - 1, -1, -1):
                    if far or off:
                        action((across[off], along[far]))
        else:
            @pl.loop(1, total)
            def _(step):
                other = lax.rem(me + step, total)
                action((other // members, lax.rem(other, members)))

    inverse_rows[...] = jnp.zeros(inverse_rows.shape, F32)
    face_in[...] = jnp.zeros(face_in.shape, F32)
    halo_in[...] = jnp.zeros(halo_in.shape, F32)

    barrier = pltpu.get_barrier_semaphore()

    each_peer(
        lambda where: pl.semaphore_signal(barrier, inc=1, device_id=where, device_id_type=pl.DeviceIdType.MESH)
    )
    for copy in loads[:-1]:
        copy.wait()
    tables(
        live_own, face_count_own.at[0], load, dof_map_own.at[0], dof_sign_own.at[0], face_slot_own.at[0],
        coord_own.at[0], pack, unpack, slots, mask, weight, modes, face_modes, rhs,
    )
    coarse_layout(raw_own, coarse, groups, members)
    pl.semaphore_wait(barrier, total - 1)

    def remote(src, dst, send, recv, where):
        return pltpu.make_async_remote_copy(
            src_ref=src, dst_ref=dst, send_sem=send, recv_sem=recv,
            device_id=where, device_id_type=pl.DeviceIdType.MESH,
        )

    def sided(ref, way):
        if way == LEFT:
            return ref.at[0]
        return ref.at[1] if way == RIGHT else ref

    def halo_copy(turn, way):
        to = opposite[way]
        return remote(
            sided(halo_out.at[turn], way), sided(halo_in.at[turn, to], way),
            send_halo.at[turn, way], recv_halo.at[turn, to], neighbours[way][1],
        )

    def face_copy(way):
        to = opposite[way]
        return remote(
            sided(face_modes, way), sided(face_in.at[to], way),
            send_setup.at[0, way], recv_setup.at[0, to], neighbours[way][1],
        )

    def coarse_copy(way):
        to = opposite[way]
        return remote(
            sided(coarse, way),
            (inverse_rows.at[2, 1], inverse_rows.at[1, 0], inverse_rows.at[4], inverse_rows.at[3])[way],
            send_setup.at[1, way], recv_setup.at[1, to], neighbours[way][1],
        )

    def each_way(action):
        for way in range(4):
            @pl.when(neighbours[way][0])
            def _():
                action(way)

    def gather_start(turn, row):
        gather_out[turn] = row
        gather_in[turn, me] = row

        each_peer(
            lambda where: remote(
                gather_out.at[turn], gather_in.at[turn, me],
                send_gather.at[turn], recv_gather.at[turn], where,
            ).start()
        )

    def gather_view(turn):
        return gather_in.at[turn, pl.ds(0, total - 1)]

    def gather_wait(turn):
        view = gather_view(turn)
        pltpu.make_async_copy(view, view, recv_gather.at[turn]).wait()

    lane_row = iota((1, message), 1)

    def placing(s):
        at = iota((40, message), 0)
        lane = iota((40, message), 1)
        kind, a = at >> 3, at & 7
        own = 16 * c + 8 * s
        to_left = own - 8 if s == 1 else span + 16 * c + 8
        to_right = own + 8 if s == 0 else span + 16 * c
        base = jnp.where(kind == 0, own, jnp.where(kind == 1, to_left, jnp.where(
            kind == 2, to_right, jnp.where(kind == 3, own - 16, own + 16))))
        return jnp.where((lane == base + a) & (a < 6), 1.0, 0.0)

    places = [placing(s) for s in range(subs)]

    def coarse_sum(turn):
        summed = jnp.sum(gather_in[turn].reshape(groups, members, 1, message), axis=0).reshape(members, message)
        if span >= TILE:
            low, high = summed[:, :span], summed[:, span : 2 * span]
        else:
            lane = iota((members, message), 1)
            low = jnp.where(lane < span, summed, 0.0)
            high = jnp.where(lane < span, pltpu.roll(summed, message - span, 1), 0.0)
        second = ((iota((members, width), 1) >> 3) & 1) == 1
        none = jnp.zeros((1, width), F32)
        from_right = jnp.concatenate([high[1:], none], axis=0)
        from_left = jnp.concatenate([none, high[:-1]], axis=0)
        return low + jnp.where(second, from_right, from_left)

    def correction(coarse_values):
        fields = []
        for s in range(subs):
            spread = jnp.zeros((8, size), F32)
            for kind in range(5):
                product = jnp.zeros((8, width), F32)
                for at in range(members):
                    product = product + inverse_rows[kind, s, at] * coarse_values[at : at + 1, :]
                alpha = jnp.sum(product, axis=1, keepdims=True)
                spread = spread + shape_rows[s, 8 * kind : 8 * kind + 8, :] * alpha
            fields.append(jnp.sum(spread, axis=0, keepdims=True))
        return fields

    def apply_dual(fields):
        images = []
        for s in range(subs):
            sums = [jnp.zeros((8, TILE), F32) for _ in range(size // TILE)]
            for b in range(size // TILE):
                reach = (b + 1) * TILE
                panel = linv[s, b * TILE : reach, :reach]
                column = jnp.sum(panel * fields[s][:, :reach], axis=1, keepdims=True)
                for at in range(b + 1):
                    piece = panel[:, at * TILE : (at + 1) * TILE] * column
                    sums[at] = sums[at] + jnp.sum(piece.reshape(TILE // 8, 8, TILE), axis=0)
            image = jnp.concatenate([jnp.sum(part, axis=0, keepdims=True) for part in sums], axis=1)
            images.append(image * mask[s : s + 1, :])
        return images

    face_lane = iota((1, faces), 1)

    def from_faces(right, left, up, down):
        return jnp.where(
            face_lane < cap, right,
            jnp.where(face_lane < 2 * cap, left, jnp.where(face_lane < 3 * cap, up, down)),
        )

    def project(turn, fields, scalars):
        row = jnp.zeros((1, message), F32)
        for s in range(subs):
            column = jnp.sum(shape_rows[s] * fields[s], axis=1, keepdims=True)
            row = row + jnp.sum(places[s] * column, axis=0, keepdims=True)
        spare = (6, 7, 14)
        for at, value in enumerate(scalars):
            row = row + jnp.where(lane_row == 16 * c + spare[at], value, 0.0)
        gather_start(turn, row)
        outgoing = [row_times([fields[s]], pack[s])[0] for s in range(subs)]
        for s in range(subs):
            halo_out[turn - 1, s] = outgoing[s]
        each_way(lambda way: halo_copy(turn - 1, way).start())
        each_way(lambda way: halo_copy(turn - 1, opposite[way]).wait_recv())
        arrived = halo_in.at[turn - 1]
        rights = (outgoing[1], arrived[RIGHT, 0])
        lefts = (arrived[LEFT, 1], outgoing[0])
        assembled = []
        for s in range(subs):
            incoming = from_faces(rights[s], lefts[s], arrived[UP, s], arrived[DOWN, s])
            assembled.append(fields[s] + row_times([incoming], unpack[s])[0])
        gather_wait(turn)
        values = coarse_sum(turn)
        fixes = correction(values)
        spare_lane = iota(values.shape, 1) & 15
        sums = []
        for at in range(len(scalars)):
            kept = jnp.where(spare_lane == spare[at], values, 0.0)
            sums.append(jnp.sum(jnp.sum(kept, axis=1, keepdims=True), axis=0, keepdims=True))
        return [assembled[s] - fixes[s] for s in range(subs)], sums

    each_way(lambda way: face_copy(way).start())
    each_way(lambda way: coarse_copy(way).start())
    row = jnp.zeros((1, message), F32)
    for s in range(subs):
        column = jnp.concatenate([rhs[s][:, 0:1], jnp.zeros((32, 1), F32)], axis=0)
        row = row + jnp.sum(places[s] * column, axis=0, keepdims=True)
    gather_start(0, row)
    for s in range(subs):
        inverse_rows[0, s] = coarse[s]
    inverse_rows[2, 0] = coarse[1]
    inverse_rows[1, 1] = coarse[0]
    loads[-1].wait()
    invert(factor, linv, subs)
    each_way(lambda way: face_copy(opposite[way]).wait_recv())
    each_way(lambda way: coarse_copy(opposite[way]).wait_recv())
    rights = (face_modes[1], face_in[RIGHT, 0])
    lefts = (face_in[LEFT, 1], face_modes[0])
    block = iota((8, faces), 1) // cap
    for s in range(subs):
        sources = (lefts[s], rights[s], face_in[DOWN, s], face_in[UP, s])
        spread = jnp.concatenate(
            [jnp.where(block == (1, 0, 3, 2)[f], sources[f], 0.0) for f in range(4)], axis=0
        ).astype(BF16)
        shape_rows[s, 0:8, :] = modes[s]
        shape_rows[s, 8:40, :] = dot(spread, unpack[s])
    gather_wait(0)
    multipliers = correction(coarse_sum(0))
    start = apply_dual([load[s : s + 1, :] - multipliers[s] for s in range(subs)])
    projected, _ = project(1, start, [])
    for turn in range(ITERS):
        image = apply_dual(projected)
        norm = sum(
            jnp.sum(weight[s : s + 1, :] * projected[s] * projected[s], axis=1, keepdims=True) for s in range(subs)
        )
        energy = sum(jnp.sum(projected[s] * image[s], axis=1, keepdims=True) for s in range(subs))
        partials = [norm, energy]
        if turn:
            partials.append(
                sum(jnp.sum(projected[s] * direction_image[s], axis=1, keepdims=True) for s in range(subs))
            )
        change, sums = project(2 + turn, image, partials)
        if turn:
            ratio = sums[0] / norm_now
            curvature = sums[1] + 2.0 * ratio * sums[2] + ratio * ratio * curvature
            direction = [projected[s] + ratio * direction[s] for s in range(subs)]
            direction_image = [image[s] + ratio * direction_image[s] for s in range(subs)]
            direction_change = [change[s] + ratio * direction_change[s] for s in range(subs)]
        else:
            curvature = sums[1]
            direction, direction_image, direction_change = projected, image, change
        norm_now = sums[0]
        step = norm_now / curvature
        multipliers = [multipliers[s] + step * direction[s] for s in range(subs)]
        projected = [projected[s] - step * direction_change[s] for s in range(subs)]
    for s in range(subs):
        ordered = row_times([multipliers[s], projected[s]], slots[s])
        out[0, s : s + 1, :] = ordered[0]
        out[1, s : s + 1, :] = ordered[1]

    each_way(lambda way: face_copy(way).wait_send())
    each_way(lambda way: coarse_copy(way).wait_send())
    for turn in range(ITERS + 1):
        each_way(lambda way: halo_copy(turn, way).wait_send())
    for turn in range(ITERS + 2):
        view = gather_view(turn)
        pltpu.make_async_copy(view, view, send_gather.at[turn]).wait()


def shards(
    groups, members,
    factor, load, dof_map, dof_sign, live_count, face_slot, face_count, node_coord, coarse_inverse,
):
    subs, size = load.shape[1:]
    faces = 4 * face_slot.shape[3]
    span = 16 * groups
    width = -(-span // TILE) * TILE
    message = -(-2 * span // TILE) * TILE
    args = (
        factor, load, dof_map, dof_sign, live_count, face_slot, face_count, node_coord.transpose(0, 2, 1, 3), coarse_inverse
    )
    shape = jax.ShapeDtypeStruct
    turns = ITERS + 2
    result = pl.pallas_call(
        functools.partial(pcg_kernel, groups, members),
        name="pcg",
        out_shape=shape((2, subs, size), F32),
        in_specs=[pl.BlockSpec(memory_space=pltpu.HBM)] * len(args),
        out_specs=pl.BlockSpec(memory_space=pltpu.VMEM),
        scratch_shapes=[pltpu.VMEM(value.shape, value.dtype) for value in args]
        + [
            pltpu.VMEM((subs, size, size), F32),
            pltpu.VMEM((subs, size, faces), BF16),
            pltpu.VMEM((subs, faces, size), BF16),
            pltpu.VMEM((subs, size, size), BF16),
            pltpu.VMEM((subs, size), F32),
            pltpu.VMEM((subs, size), F32),
            pltpu.VMEM((subs, 8, size), F32),
            pltpu.VMEM((subs, 8, faces), F32),
            pltpu.VMEM((subs, 8, TILE), F32),
            pltpu.VMEM((subs, members, 8, width), F32),
            pltpu.SemaphoreType.DMA((len(args),)),
            pltpu.VMEM((5, subs, members, 8, width), F32),
            pltpu.VMEM((4, subs, 8, faces), F32),
            pltpu.VMEM((subs, 40, size), F32),
            pltpu.VMEM((turns, groups * members, 1, message), F32),
            pltpu.VMEM((turns, 1, message), F32),
            pltpu.VMEM((turns - 1, 4, subs, 1, faces), F32),
            pltpu.VMEM((turns - 1, subs, 1, faces), F32),
            pltpu.SemaphoreType.DMA((turns,)),
            pltpu.SemaphoreType.DMA((turns,)),
            pltpu.SemaphoreType.DMA((turns - 1, 4)),
            pltpu.SemaphoreType.DMA((turns - 1, 4)),
            pltpu.SemaphoreType.DMA((2, 4)),
            pltpu.SemaphoreType.DMA((2, 4)),
        ],
        compiler_params=pltpu.CompilerParams(
            collective_id=0, has_side_effects=True, vmem_limit_bytes=VMEM_LIMIT
        ),
    )(*args)
    return result[0:1], result[1:2]


def solution(mesh):
    return jax.shard_map(
        functools.partial(shards, mesh.shape["group"], mesh.shape["member"]),
        mesh=mesh,
        in_specs=(
            P("group", "member", None, None),
            P("group", "member", None),
            P("group", "member", None),
            P("group", "member", None),
            P("group", "member"),
            P("group", "member", None, None),
            P("group", "member", None),
            P("group", "member", None, None),
            P(("group", "member"), None),
        ),
        out_specs=(P("group", "member", None), P("group", "member", None)),
        check_vma=False,
    )
```

```python
import functools

import jax
import jax.numpy as jnp
from jax import lax
from jax.experimental import pallas as pl
from jax.experimental.pallas import tpu as pltpu
from jax.sharding import PartitionSpec as P

ITERS = 3
BASE = 16
TILE = 128
HALF_SPAN = 8.0
VMEM_LIMIT = 62 * 2**20
LEFT, RIGHT, DOWN, UP = range(4)
F32 = jnp.float32
BF16 = jnp.bfloat16
NN = (((1,), (0,)), ((), ()))


def iota(shape, dim):
    return lax.broadcasted_iota(jnp.int32, shape, dim)


def dot(left, right, dims=NN):
    return lax.dot_general(left, right, dims, preferred_element_type=F32)


def parts_of(values, count):
    parts = []
    for _ in range(count):
        part = values.astype(BF16)
        parts.append(part)
        values = values - part.astype(F32)
    return parts


def mm(left, right):
    left_hi, left_lo = parts_of(left, 2)
    right_hi, right_lo = parts_of(right, 2)
    if left.shape[1] == TILE:
        deep = dot(
            jnp.concatenate([left_hi, left_lo], axis=1), jnp.concatenate([right_hi, right_hi], axis=0)
        )
        return deep + dot(left_hi, right_lo)
    return dot(left_hi, right_hi) + (dot(left_hi, right_lo) + dot(left_lo, right_hi))


def row_times(rows, table, dims=NN):
    stacked = []
    for row in rows:
        for part in parts_of(row, 3):
            stacked.append(part.astype(F32))
    pad = -len(stacked) % 8
    stacked.append(jnp.zeros((pad, rows[0].shape[1]), F32))
    product = dot(jnp.concatenate(stacked, axis=0).astype(BF16), table, dims)
    return [
        product[3 * at : 3 * at + 1] + product[3 * at + 1 : 3 * at + 2] + product[3 * at + 2 : 3 * at + 3]
        for at in range(len(rows))
    ]


def invert(factor, linv, subs):
    size = factor.shape[1]
    blocks = size // TILE
    row = iota((TILE, TILE), 0)
    lane = iota((TILE, TILE), 1)
    shift = BASE.bit_length() - 1
    same = (row >> shift) == (lane >> shift)
    where_at = [(s, b) for s in range(subs) for b in range(blocks)]

    def diagonal(s, b):
        return factor[s, b * TILE : (b + 1) * TILE, b * TILE : (b + 1) * TILE]

    packed = []
    for s, b in where_at:
        kept = jnp.where(same, diagonal(s, b), 0.0)
        packed.append(jnp.sum(kept.reshape(TILE // BASE, BASE, TILE), axis=0))
    count = len(packed)
    packed = jnp.concatenate(packed, axis=0)
    wide = (TILE, BASE * TILE)
    source, target = iota(wide, 0), iota(wide, 1)
    spread = (((source & (BASE - 1)) == (target >> 7)) & ((source >> shift) == ((target & 127) >> shift)))
    spread = jnp.where(spread, 1.0, 0.0).astype(BF16)
    high, middle, low = parts_of(packed, 3)
    columns = dot(
        jnp.concatenate([high, middle], axis=1), jnp.concatenate([spread, spread], axis=0)
    ) + dot(low, spread)
    within = iota((count, BASE, TILE), 1)
    solved = jnp.where(within == (iota((count, BASE, TILE), 2) & (BASE - 1)), 1.0, 0.0)
    for m in range(BASE):
        column = columns[:, m * TILE : (m + 1) * TILE].reshape(count, BASE, TILE)
        pivot = solved[:, m : m + 1, :] / column[:, m : m + 1, :]
        solved = jnp.where(within > m, solved - column * pivot, jnp.where(within == m, pivot, solved))
    inverses = [
        jnp.where(same, jnp.concatenate([solved[at]] * (TILE // BASE), axis=0), 0.0) for at in range(count)
    ]
    width = BASE
    while width < TILE:
        level = width.bit_length() - 1
        below = (
            ((row >> (level + 1)) == (lane >> (level + 1)))
            & (((row >> level) & 1) == 1)
            & (((lane >> level) & 1) == 0)
        )
        middle = [
            mm(jnp.where(below, diagonal(s, b), 0.0), inverses[at]) for at, (s, b) in enumerate(where_at)
        ]
        inverses = [inverses[at] - mm(inverses[at], middle[at]) for at in range(count)]
        width *= 2
    for at, (s, b) in enumerate(where_at):
        rows = slice(b * TILE, (b + 1) * TILE)
        linv[s, rows, rows] = inverses[at]
        if b + 1 < blocks:
            linv[s, rows, (b + 1) * TILE :] = jnp.zeros((TILE, size - (b + 1) * TILE), F32)
    width = TILE
    while width < size:
        for start in range(0, size - width, 2 * width):
            middle_at, end = start + width, min(start + 2 * width, size)
            for s in range(subs):
                upper = linv[s, start:middle_at, start:middle_at]
                lower = linv[s, middle_at:end, middle_at:end]
                linv[s, middle_at:end, start:middle_at] = -mm(lower, mm(factor[s, middle_at:end, start:middle_at], upper))
        width *= 2


def tables(
    live, face_count, load, dof_map, dof_sign, face_slot, coord,
    pack, unpack, slots, mask, weight, modes, face_modes, rhs,
):
    subs, size = load.shape
    cap = face_slot.shape[2]
    nodes = coord.shape[2]
    for s in range(subs):
        sign_row = jnp.where(iota((1, size), 1) < live[0:1, s : s + 1], dof_sign[s : s + 1, :].astype(F32), 0.0)
        slot_rows = jnp.where(iota((size, size), 0) == dof_map[s : s + 1, :], sign_row, 0.0).astype(BF16)
        slots[s] = slot_rows

        def hits(order):
            face_row = jnp.concatenate([face_slot[s, f : f + 1, :] for f in order], axis=1)
            lane = iota((1, 4 * cap), 1)
            limit = jnp.zeros((1, 4 * cap), jnp.int32)
            for at, f in enumerate(order):
                limit = jnp.where(lane // cap == at, at * cap + face_count[s : s + 1, f : f + 1], limit)
            face_row = jnp.where(lane < limit, face_row, -1)
            return jnp.where(iota((size, 4 * cap), 0) == face_row, 1.0, 0.0).astype(BF16)

        sign_column = jnp.broadcast_to(sign_row, (TILE, size)).T.astype(BF16)
        product = dot(
            slot_rows, jnp.concatenate([hits((0, 1, 2, 3)), hits((1, 0, 3, 2)), sign_column], axis=1)
        )
        outgoing = product[:, : 4 * cap].astype(BF16)
        pack[s] = outgoing
        turned = product[:, 4 * cap :].T
        unpack[s] = turned[: 4 * cap].astype(BF16)
        live_row = turned[4 * cap : 4 * cap + 1]
        shared = jnp.sum(jnp.abs(turned[: 4 * cap]), axis=0, keepdims=True)
        mask[s : s + 1, :] = live_row
        weight[s : s + 1, :] = live_row * (1.0 - 0.5 * shared)
        position = jnp.concatenate([coord[axis, s : s + 1, :] for axis in range(3)], axis=0)
        position = (position.astype(F32) - HALF_SPAN) / HALF_SPAN
        stacked = jnp.concatenate(
            [position, iota((1, nodes), 1).astype(F32), jnp.zeros((4, nodes), F32)], axis=0
        ).astype(BF16)
        first_of = 3 * iota((nodes, size), 0)
        unknown = iota((nodes, size), 1)
        of_node = jnp.where((unknown >= first_of) & (unknown < first_of + 3), 1.0, 0.0).astype(BF16)
        spread = dot(stacked, of_node)
        x, y, z = spread[0:1], spread[1:2], spread[2:3]
        component = iota((1, size), 1).astype(F32) - 3.0 * spread[3:4]
        first = jnp.where(component == 0.0, 1.0, 0.0)
        second = jnp.where(component == 1.0, 1.0, 0.0)
        third = jnp.where(component == 2.0, 1.0, 0.0)
        table = jnp.concatenate(
            [
                first,
                second,
                third,
                third * y - second * z,
                first * z - third * x,
                second * x - first * y,
                jnp.zeros((2, size), F32),
            ],
            axis=0,
        )
        modes[s] = table * live_row
        face_modes[s] = dot(table.astype(BF16), outgoing)
        rhs[s] = jnp.broadcast_to(jnp.sum(table * load[s : s + 1, :], axis=1, keepdims=True), (8, TILE))


def coarse_layout(raw, coarse, groups, members):
    width = coarse.shape[-1]
    none = jnp.zeros((2, raw.shape[1]), F32)
    rows = jnp.concatenate([raw[0:6, :], none, raw[6:12, :], none], axis=0)
    stacked = jnp.concatenate([part.astype(F32) for part in parts_of(rows, 3)], axis=0).astype(BF16)

    def one(at, carry):
        lane = iota((1, width), 1)
        column = 12 * ((lane >> 4) * members + at) + 6 * ((lane >> 3) & 1) + (lane & 7)
        column = jnp.where(((lane & 7) < 6) & (lane < 16 * groups), column, -1)
        pick = jnp.where(iota((raw.shape[1], width), 0) == column, 1.0, 0.0).astype(BF16)
        picked = dot(stacked, pick)
        picked = picked[0:16] + picked[16:32] + picked[32:48]
        coarse[0, at] = picked[0:8]
        coarse[1, at] = picked[8:16]
        return carry

    lax.fori_loop(0, members, one, 0, unroll=members <= 8)


def pcg_kernel(
    groups, members,
    factor_hbm, load_hbm, dof_map_hbm, dof_sign_hbm, live_hbm, face_slot_hbm, face_count_hbm, coord_hbm, raw_hbm,
    out,
    factor_own, load_own, dof_map_own, dof_sign_own, live_own, face_slot_own, face_count_own, coord_own, raw_own,
    linv, pack, unpack, slots, mask, weight, modes, face_modes, rhs, coarse, load_sem,
    inverse_rows, face_in, shape_rows, gather_in, gather_out, halo_in, halo_out,
    send_gather, recv_gather, send_halo, recv_halo, send_setup, recv_setup,
):
    loads = [
        pltpu.make_async_copy(src, dst, load_sem.at[at])
        for at, (src, dst) in enumerate((
            (load_hbm, load_own), (dof_map_hbm, dof_map_own), (dof_sign_hbm, dof_sign_own),
            (live_hbm, live_own), (face_slot_hbm, face_slot_own), (face_count_hbm, face_count_own),
            (coord_hbm, coord_own), (raw_hbm, raw_own), (factor_hbm, factor_own),
        ))
    ]
    for copy in loads:
        copy.start()
    factor, load = factor_own.at[0], load_own.at[0]
    subs, size = load.shape
    faces = pack.shape[2]
    cap = faces // 4
    total = groups * members
    span = 16 * groups
    width = coarse.shape[-1]
    message = gather_out.shape[-1]
    c, m = lax.axis_index("group"), lax.axis_index("member")
    me = c * members + m
    neighbours = (
        (m > 0, (c, lax.rem(m + members - 1, members))),
        (m < members - 1, (c, lax.rem(m + 1, members))),
        (c > 0, (lax.rem(c + groups - 1, groups), m)),
        (c < groups - 1, (lax.rem(c + 1, groups), m)),
    )
    opposite = (RIGHT, LEFT, UP, DOWN)

    across = [lax.rem(c + step, groups) for step in range(groups)]
    along = [lax.rem(m + step, members) for step in range(members)]

    def each_peer(action):
        if total <= 32:
            for far in range(members - 1, -1, -1):
                for off in range(groups - 1, -1, -1):
                    if far or off:
                        action((across[off], along[far]))
        else:
            @pl.loop(1, total)
            def _(step):
                other = lax.rem(me + step, total)
                action((other // members, lax.rem(other, members)))

    inverse_rows[...] = jnp.zeros(inverse_rows.shape, F32)
    face_in[...] = jnp.zeros(face_in.shape, F32)
    halo_in[...] = jnp.zeros(halo_in.shape, F32)

    barrier = pltpu.get_barrier_semaphore()

    each_peer(
        lambda where: pl.semaphore_signal(barrier, inc=1, device_id=where, device_id_type=pl.DeviceIdType.MESH)
    )
    for copy in loads[:-1]:
        copy.wait()
    tables(
        live_own, face_count_own.at[0], load, dof_map_own.at[0], dof_sign_own.at[0], face_slot_own.at[0],
        coord_own.at[0], pack, unpack, slots, mask, weight, modes, face_modes, rhs,
    )
    coarse_layout(raw_own, coarse, groups, members)
    pl.semaphore_wait(barrier, total - 1)

    def remote(src, dst, send, recv, where):
        return pltpu.make_async_remote_copy(
            src_ref=src, dst_ref=dst, send_sem=send, recv_sem=recv,
            device_id=where, device_id_type=pl.DeviceIdType.MESH,
        )

    def sided(ref, way):
        if way == LEFT:
            return ref.at[0]
        return ref.at[1] if way == RIGHT else ref

    def halo_copy(turn, way):
        to = opposite[way]
        return remote(
            sided(halo_out.at[turn], way), sided(halo_in.at[turn, to], way),
            send_halo.at[turn, way], recv_halo.at[turn, to], neighbours[way][1],
        )

    def face_copy(way):
        to = opposite[way]
        return remote(
            sided(face_modes, way), sided(face_in.at[to], way),
            send_setup.at[0, way], recv_setup.at[0, to], neighbours[way][1],
        )

    def coarse_copy(way):
        to = opposite[way]
        return remote(
            sided(coarse, way),
            (inverse_rows.at[2, 1], inverse_rows.at[1, 0], inverse_rows.at[4], inverse_rows.at[3])[way],
            send_setup.at[1, way], recv_setup.at[1, to], neighbours[way][1],
        )

    def each_way(action):
        for way in range(4):
            @pl.when(neighbours[way][0])
            def _():
                action(way)

    def gather_start(turn, row):
        gather_out[turn] = row
        gather_in[turn, me] = row

        each_peer(
            lambda where: remote(
                gather_out.at[turn], gather_in.at[turn, me],
                send_gather.at[turn], recv_gather.at[turn], where,
            ).start()
        )

    def gather_view(turn):
        return gather_in.at[turn, pl.ds(0, total - 1)]

    def gather_wait(turn):
        view = gather_view(turn)
        pltpu.make_async_copy(view, view, recv_gather.at[turn]).wait()

    lane_row = iota((1, message), 1)

    def placing(s):
        at = iota((40, message), 0)
        lane = iota((40, message), 1)
        kind, a = at >> 3, at & 7
        own = 16 * c + 8 * s
        to_left = own - 8 if s == 1 else span + 16 * c + 8
        to_right = own + 8 if s == 0 else span + 16 * c
        base = jnp.where(kind == 0, own, jnp.where(kind == 1, to_left, jnp.where(
            kind == 2, to_right, jnp.where(kind == 3, own - 16, own + 16))))
        return jnp.where((lane == base + a) & (a < 6), 1.0, 0.0)

    places = [placing(s) for s in range(subs)]

    def coarse_sum(turn):
        summed = jnp.sum(gather_in[turn].reshape(groups, members, 1, message), axis=0).reshape(members, message)
        if span >= TILE:
            low, high = summed[:, :span], summed[:, span : 2 * span]
        else:
            lane = iota((members, message), 1)
            low = jnp.where(lane < span, summed, 0.0)
            high = jnp.where(lane < span, pltpu.roll(summed, message - span, 1), 0.0)
        second = ((iota((members, width), 1) >> 3) & 1) == 1
        none = jnp.zeros((1, width), F32)
        from_right = jnp.concatenate([high[1:], none], axis=0)
        from_left = jnp.concatenate([none, high[:-1]], axis=0)
        return low + jnp.where(second, from_right, from_left)

    def correction(coarse_values):
        fields = []
        for s in range(subs):
            spread = jnp.zeros((8, size), F32)
            for kind in range(5):
                product = jnp.zeros((8, width), F32)
                for at in range(members):
                    product = product + inverse_rows[kind, s, at] * coarse_values[at : at + 1, :]
                alpha = jnp.sum(product, axis=1, keepdims=True)
                spread = spread + shape_rows[s, 8 * kind : 8 * kind + 8, :] * alpha
            fields.append(jnp.sum(spread, axis=0, keepdims=True))
        return fields

    def apply_dual(fields):
        images = []
        for s in range(subs):
            sums = [jnp.zeros((8, TILE), F32) for _ in range(size // TILE)]
            for b in range(size // TILE):
                reach = (b + 1) * TILE
                panel = linv[s, b * TILE : reach, :reach]
                column = jnp.sum(panel * fields[s][:, :reach], axis=1, keepdims=True)
                for at in range(b + 1):
                    piece = panel[:, at * TILE : (at + 1) * TILE] * column
                    sums[at] = sums[at] + jnp.sum(piece.reshape(TILE // 8, 8, TILE), axis=0)
            image = jnp.concatenate([jnp.sum(part, axis=0, keepdims=True) for part in sums], axis=1)
            images.append(image * mask[s : s + 1, :])
        return images

    face_lane = iota((1, faces), 1)

    def from_faces(right, left, up, down):
        return jnp.where(
            face_lane < cap, right,
            jnp.where(face_lane < 2 * cap, left, jnp.where(face_lane < 3 * cap, up, down)),
        )

    def project(turn, fields, scalars):
        row = jnp.zeros((1, message), F32)
        for s in range(subs):
            column = jnp.sum(shape_rows[s] * fields[s], axis=1, keepdims=True)
            row = row + jnp.sum(places[s] * column, axis=0, keepdims=True)
        spare = (6, 7, 14)
        for at, value in enumerate(scalars):
            row = row + jnp.where(lane_row == 16 * c + spare[at], value, 0.0)
        gather_start(turn, row)
        outgoing = [row_times([fields[s]], pack[s])[0] for s in range(subs)]
        for s in range(subs):
            halo_out[turn - 1, s] = outgoing[s]
        each_way(lambda way: halo_copy(turn - 1, way).start())
        each_way(lambda way: halo_copy(turn - 1, opposite[way]).wait_recv())
        arrived = halo_in.at[turn - 1]
        rights = (outgoing[1], arrived[RIGHT, 0])
        lefts = (arrived[LEFT, 1], outgoing[0])
        assembled = []
        for s in range(subs):
            incoming = from_faces(rights[s], lefts[s], arrived[UP, s], arrived[DOWN, s])
            assembled.append(fields[s] + row_times([incoming], unpack[s])[0])
        gather_wait(turn)
        values = coarse_sum(turn)
        fixes = correction(values)
        spare_lane = iota(values.shape, 1) & 15
        sums = []
        for at in range(len(scalars)):
            kept = jnp.where(spare_lane == spare[at], values, 0.0)
            sums.append(jnp.sum(jnp.sum(kept, axis=1, keepdims=True), axis=0, keepdims=True))
        return [assembled[s] - fixes[s] for s in range(subs)], sums

    each_way(lambda way: face_copy(way).start())
    each_way(lambda way: coarse_copy(way).start())
    row = jnp.zeros((1, message), F32)
    for s in range(subs):
        column = jnp.concatenate([rhs[s][:, 0:1], jnp.zeros((32, 1), F32)], axis=0)
        row = row + jnp.sum(places[s] * column, axis=0, keepdims=True)
    gather_start(0, row)
    for s in range(subs):
        inverse_rows[0, s] = coarse[s]
    inverse_rows[2, 0] = coarse[1]
    inverse_rows[1, 1] = coarse[0]
    loads[-1].wait()
    invert(factor, linv, subs)
    each_way(lambda way: face_copy(opposite[way]).wait_recv())
    each_way(lambda way: coarse_copy(opposite[way]).wait_recv())
    rights = (face_modes[1], face_in[RIGHT, 0])
    lefts = (face_in[LEFT, 1], face_modes[0])
    block = iota((8, faces), 1) // cap
    for s in range(subs):
        sources = (lefts[s], rights[s], face_in[DOWN, s], face_in[UP, s])
        spread = jnp.concatenate(
            [jnp.where(block == (1, 0, 3, 2)[f], sources[f], 0.0) for f in range(4)], axis=0
        ).astype(BF16)
        shape_rows[s, 0:8, :] = modes[s]
        shape_rows[s, 8:40, :] = dot(spread, unpack[s])
    gather_wait(0)
    multipliers = correction(coarse_sum(0))
    start = apply_dual([load[s : s + 1, :] - multipliers[s] for s in range(subs)])
    projected, _ = project(1, start, [])
    for turn in range(ITERS):
        image = apply_dual(projected)
        norm = sum(
            jnp.sum(weight[s : s + 1, :] * projected[s] * projected[s], axis=1, keepdims=True) for s in range(subs)
        )
        energy = sum(jnp.sum(projected[s] * image[s], axis=1, keepdims=True) for s in range(subs))
        partials = [norm, energy]
        if turn:
            partials.append(
                sum(jnp.sum(projected[s] * direction_image[s], axis=1, keepdims=True) for s in range(subs))
            )
        change, sums = project(2 + turn, image, partials)
        if turn:
            ratio = sums[0] / norm_now
            curvature = sums[1] + 2.0 * ratio * sums[2] + ratio * ratio * curvature
            direction = [projected[s] + ratio * direction[s] for s in range(subs)]
            direction_image = [image[s] + ratio * direction_image[s] for s in range(subs)]
            direction_change = [change[s] + ratio * direction_change[s] for s in range(subs)]
        else:
            curvature = sums[1]
            direction, direction_image, direction_change = projected, image, change
        norm_now = sums[0]
        step = norm_now / curvature
        multipliers = [multipliers[s] + step * direction[s] for s in range(subs)]
        projected = [projected[s] - step * direction_change[s] for s in range(subs)]
    for s in range(subs):
        ordered = row_times([multipliers[s], projected[s]], slots[s])
        out[0, s : s + 1, :] = ordered[0]
        out[1, s : s + 1, :] = ordered[1]

    each_way(lambda way: face_copy(way).wait_send())
    each_way(lambda way: coarse_copy(way).wait_send())
    for turn in range(ITERS + 1):
        each_way(lambda way: halo_copy(turn, way).wait_send())
    for turn in range(ITERS + 2):
        view = gather_view(turn)
        pltpu.make_async_copy(view, view, send_gather.at[turn]).wait()


def shards(
    groups, members,
    factor, load, dof_map, dof_sign, live_count, face_slot, face_count, node_coord, coarse_inverse,
):
    subs, size = load.shape[1:]
    faces = 4 * face_slot.shape[3]
    span = 16 * groups
    width = -(-span // TILE) * TILE
    message = -(-2 * span // TILE) * TILE
    args = (
        factor, load, dof_map, dof_sign, live_count, face_slot, face_count, node_coord.transpose(0, 2, 1, 3), coarse_inverse
    )
    shape = jax.ShapeDtypeStruct
    turns = ITERS + 2
    result = pl.pallas_call(
        functools.partial(pcg_kernel, groups, members),
        name="pcg",
        out_shape=shape((2, subs, size), F32),
        in_specs=[pl.BlockSpec(memory_space=pltpu.HBM)] * len(args),
        out_specs=pl.BlockSpec(memory_space=pltpu.VMEM),
        scratch_shapes=[pltpu.VMEM(value.shape, value.dtype) for value in args]
        + [
            pltpu.VMEM((subs, size, size), F32),
            pltpu.VMEM((subs, size, faces), BF16),
            pltpu.VMEM((subs, faces, size), BF16),
            pltpu.VMEM((subs, size, size), BF16),
            pltpu.VMEM((subs, size), F32),
            pltpu.VMEM((subs, size), F32),
            pltpu.VMEM((subs, 8, size), F32),
            pltpu.VMEM((subs, 8, faces), F32),
            pltpu.VMEM((subs, 8, TILE), F32),
            pltpu.VMEM((subs, members, 8, width), F32),
            pltpu.SemaphoreType.DMA((len(args),)),
            pltpu.VMEM((5, subs, members, 8, width), F32),
            pltpu.VMEM((4, subs, 8, faces), F32),
            pltpu.VMEM((subs, 40, size), F32),
            pltpu.VMEM((turns, groups * members, 1, message), F32),
            pltpu.VMEM((turns, 1, message), F32),
            pltpu.VMEM((turns - 1, 4, subs, 1, faces), F32),
            pltpu.VMEM((turns - 1, subs, 1, faces), F32),
            pltpu.SemaphoreType.DMA((turns,)),
            pltpu.SemaphoreType.DMA((turns,)),
            pltpu.SemaphoreType.DMA((turns - 1, 4)),
            pltpu.SemaphoreType.DMA((turns - 1, 4)),
            pltpu.SemaphoreType.DMA((2, 4)),
            pltpu.SemaphoreType.DMA((2, 4)),
        ],
        compiler_params=pltpu.CompilerParams(
            collective_id=0, has_side_effects=True, vmem_limit_bytes=VMEM_LIMIT
        ),
    )(*args)
    return result[0:1], result[1:2]


def solution(mesh):
    return jax.shard_map(
        functools.partial(shards, mesh.shape["group"], mesh.shape["member"]),
        mesh=mesh,
        in_specs=(
            P("group", "member", None, None),
            P("group", "member", None),
            P("group", "member", None),
            P("group", "member", None),
            P("group", "member"),
            P("group", "member", None, None),
            P("group", "member", None),
            P("group", "member", None, None),
            P(("group", "member"), None),
        ),
        out_specs=(P("group", "member", None), P("group", "member", None)),
        check_vma=False,
    )
```
